32 devices in a mesh: ens: 2 (over y), dom: 4 (over z), feat: 2 (over x), sub: 2 (over core).
Axes of the slice: x: 2, y: 2, z: 4, core: 2. Of those that a mesh axis runs over, the one named last changes fastest.
Arguments:
- grid_state: bfloat16 [512, 49152], P(None, ('ens', 'dom', 'sub', 'feat')), parts along dimension 1, may hold values from -6 to 6
- mesh_state: bfloat16 [512, 8192], P('feat', ('ens', 'dom', 'sub')), parts along dimension 1, may hold values from -6 to 6
- enc_first: bfloat16 [512, 512], P('feat'), may hold values from -0.25 to 0.25
- enc_second: bfloat16 [512, 512], P('feat'), may hold values from -0.25 to 0.25
- dec_first: bfloat16 [512, 512], P('feat'), may hold values from -0.25 to 0.25
- dec_second: bfloat16 [512, 512], P('feat'), may hold values from -0.25 to 0.25
- mesh_weight: bfloat16 [512, 512], P('feat'), may hold values from -0.25 to 0.25
- send_grid: int32 [16, 2, 8, 2], P(('ens', 'dom', 'sub'), 'feat'), parts along dimension 0, may hold values from 0 to 24, as said below
- enc_tiles: bfloat16 [16, 2, 64, 1024], P(('ens', 'dom', 'sub'), 'feat'), parts along dimension 0, may hold values from -0.375 to 0.375
- enc_target: int32 [16, 2, 16], P(('ens', 'dom', 'sub'), 'feat'), parts along dimension 0, may hold values from 0 to 7
- send_mesh: int32 [16, 2, 8, 2], P(('ens', 'dom', 'sub'), 'feat'), parts along dimension 0, may hold values from 0 to 8, as said below
- dec_slots: int32 [768, 4], P(('ens', 'dom', 'sub', 'feat')), parts along dimension 0, may hold values from 0 to 15, as said below
- dec_tiles: bfloat16 [768, 64, 256], P(('ens', 'dom', 'sub', 'feat')), parts along dimension 0, may hold values from -0.375 to 0.375
Outputs:
- grid_next: bfloat16 [512, 49152], P(None, ('ens', 'dom', 'sub', 'feat')), parts along dimension 1
The draws below stay inside these ranges and needn't reach their ends.
There are 2 independent parts, one for each index of `ens`. The reference program is written for one: setup_inputs(seed, part) draws one part's arguments, and reference() takes and returns one part's arrays. A program takes and returns all parts, laid end to end along the dimension named above; an argument that names none is the same for every part. Nothing has to cross between parts.
Inputs may be any that keep to these rules, and one draw needn't show every extreme that they name: `send_grid`: the value 24 marks an empty slot; every device fills all 2 slots toward its own mesh share, and other slots are filled from the first one on. `send_mesh`: the value 8 marks an empty slot; every device fills all 2 slots toward its own grid share, and other slots are filled from the first one on. `dec_slots`: each entry names a slot of the receiving device whose send_mesh entry is not empty.
All inputs are finite; a program needn't handle non-finite values.
Results may differ from the reference program's by a relative error of at most 0.006.
Values may be sent and summed in bfloat16 or wider, within the bound.
No kernel may reach another device: no remote copies, remote signals or barrier semaphores. Data moves between devices by JAX's collectives and lax.ppermute only.
A program may use at most 64 MiB of HBM per device.

```python
import jax
import jax.numpy as jnp
from jax import lax

D = 512
BLOCK = 64
GB_DEV = 24
MB_DEV = 8
CAP = 2
CAP2 = 2
J = 4
PEERS = 8
UNITS = 16
NG = 24576
NM = 4096
N_FEAT = 2
N_SUB = 2


def pair_counts(key, slot_cap):
    key = jax.random.fold_in(key, 11)
    band_of = jnp.arange(PEERS, dtype=jnp.int32) // N_SUB
    distance = jnp.abs(band_of[:, None, None] - band_of[None, None, :])
    near_count = jax.random.randint(key, (PEERS, N_FEAT, PEERS), 1, slot_cap + 1)
    rare_far = (jax.random.randint(jax.random.fold_in(key, 2), (PEERS, N_FEAT, PEERS), 0, 4) == 0).astype(jnp.int32)
    heavy_rows = (jax.random.randint(jax.random.fold_in(key, 1), (PEERS,), 0, 4) == 0).astype(jnp.int32)
    far_count = rare_far + heavy_rows[None, None, :]
    counts = jnp.minimum(jnp.where(distance <= 1, near_count, far_count), slot_cap)
    own_pair = jnp.arange(PEERS)[:, None, None] == jnp.arange(PEERS)[None, None, :]
    return jnp.where(own_pair, slot_cap, counts).astype(jnp.int32)


def fill_lists(key, counts, slot_cap, bound_val):
    entries = jax.random.randint(key, (PEERS, N_FEAT, PEERS, slot_cap), 0, bound_val)
    in_use = jnp.arange(slot_cap)[None, None, None, :] < counts[..., None]
    return jnp.where(in_use, entries, bound_val).astype(jnp.int32)


def mesh_counts(key):
    return pair_counts(jax.random.fold_in(key, 7), CAP2)


def draw_send_grid(key, part):
    key = jax.random.fold_in(key, 1)
    counts = pair_counts(jax.random.fold_in(key, 5), CAP)
    return fill_lists(jax.random.fold_in(key, 6), counts, CAP, GB_DEV)


def draw_send_mesh(key, part):
    counts = mesh_counts(key)
    key = jax.random.fold_in(key, 2)
    return fill_lists(key, counts, CAP2, MB_DEV)


def draw_dec_slots(key, part):
    counts = mesh_counts(key)
    in_use = jnp.arange(CAP2)[None, None, None, :] < counts[..., None]
    in_use = in_use.transpose(2, 1, 0, 3).reshape(UNITS, PEERS * CAP2).astype(jnp.int32)
    ranked = jnp.argsort(1 - in_use, axis=1, stable=True).astype(jnp.int32)
    valid_count = jnp.sum(in_use, axis=1)
    position = jnp.arange(GB_DEV * J, dtype=jnp.int32)[None, :] % valid_count[:, None]
    slots = jnp.take_along_axis(ranked, position, axis=1)
    return slots.reshape(UNITS * GB_DEV, J).astype(jnp.int32)


def plant(drawn, stream_key, low, largest):
    longest = drawn.shape.index(max(drawn.shape))
    spots = []
    for shift in (0, 1):
        where = [jax.random.randint(jax.random.fold_in(stream_key, axis), (), 0, length) for axis, length in enumerate(drawn.shape)]
        where[longest] = (where[longest] + shift) % drawn.shape[longest]
        spots.append(tuple(where))
    return drawn.at[spots[0]].set(low).at[spots[1]].set(largest)


def steps_of(stream_key, extent, split, low, largest):
    factor_of, own = 1.0, jax.random.fold_in(stream_key, 6)
    for axis_at, shards_of in split:
        draws = jnp.exp(jax.random.uniform(jax.random.fold_in(own, axis_at), (shards_of,), jnp.float32, low / len(split), largest / len(split)))
        factor_of = factor_of * jnp.repeat(draws, extent[axis_at] // shards_of).reshape([-1 if axis == axis_at else 1 for axis in range(len(extent))])
    return factor_of


def gaussian(stream_key, shape, deviation, most, cuts=(), kind=jnp.bfloat16):
    result = deviation * jax.random.normal(stream_key, shape, jnp.float32)
    if cuts:
        result = result * steps_of(stream_key, shape, cuts, -0.22, 0.18)
    return jnp.clip(result, -most, most).astype(kind)


def setup_inputs(seed: int = 0, part: int = 0) -> dict:
    splits = jax.random.split(jax.random.key(seed), 14)
    own_keys = jax.random.split(jax.random.fold_in(splits[13], part), 14)
    return {
        "grid_state": gaussian(own_keys[0], (D, NG), 1.0, 6.0, ((1, 16),)),
        "mesh_state": gaussian(own_keys[1], (D, NM), 1.0, 6.0, ((0, 2), (1, 8))),
        "enc_first": gaussian(splits[2], (D, D), D ** -0.5, 0.25, ((0, 2),)),
        "enc_second": gaussian(splits[3], (D, D), D ** -0.5, 0.25, ((0, 2),)),
        "dec_first": gaussian(splits[4], (D, D), D ** -0.5, 0.25, ((0, 2),)),
        "dec_second": gaussian(splits[5], (D, D), D ** -0.5, 0.25, ((0, 2),)),
        "mesh_weight": gaussian(splits[6], (D, D), D ** -0.5, 0.25, ((0, 2),)),
        "send_grid": draw_send_grid(jax.random.fold_in(jax.random.fold_in(splits[13], part), 71), part),
        "enc_tiles": gaussian(own_keys[8], (PEERS, N_FEAT, BLOCK, PEERS * CAP * BLOCK), (BLOCK * UNITS * CAP // MB_DEV) ** -0.5, 0.375, ((0, 8), (1, 2))),
        "enc_target": plant(jax.random.randint(own_keys[9], (PEERS, N_FEAT, PEERS * CAP), 0, MB_DEV), jax.random.fold_in(own_keys[9], 1), 0, MB_DEV - 1).astype(jnp.int32),
        "send_mesh": draw_send_mesh(jax.random.fold_in(jax.random.fold_in(splits[13], part), 71), part),
        "dec_slots": draw_dec_slots(jax.random.fold_in(jax.random.fold_in(splits[13], part), 71), part),
        "dec_tiles": gaussian(own_keys[12], (NG // BLOCK, BLOCK, J * BLOCK), (BLOCK * J) ** -0.5, 0.375, ((0, 16),)),
    }


def reference(grid_state, mesh_state, enc_first, enc_second, dec_first, dec_second, mesh_weight, send_grid, enc_tiles, enc_target, send_mesh, dec_slots, dec_tiles):
    grid_dev = grid_state.reshape(D, UNITS, GB_DEV * BLOCK).transpose(1, 0, 2)

    def encode(local_cols):
        hidden = jax.nn.silu(jnp.dot(enc_first.T, local_cols, preferred_element_type=jnp.float32)).astype(jnp.bfloat16)
        message = jnp.dot(enc_second.T, hidden, preferred_element_type=jnp.float32).astype(jnp.bfloat16)
        return message.reshape(D, GB_DEV, BLOCK).transpose(1, 0, 2)

    messages = lax.map(encode, grid_dev).reshape(UNITS * GB_DEV, D, BLOCK)
    grid_pool = jnp.concatenate([messages, jnp.zeros((1, D, BLOCK), jnp.bfloat16)], 0)
    source_idx = jnp.arange(PEERS, dtype=jnp.int32)[:, None, None, None]
    feat_idx = jnp.arange(N_FEAT, dtype=jnp.int32)[None, :, None, None]
    grid_ids = jnp.where(send_grid < GB_DEV, (source_idx * N_FEAT + feat_idx) * GB_DEV + send_grid, UNITS * GB_DEV).astype(jnp.int32)
    grid_ids = grid_ids.transpose(2, 1, 0, 3).reshape(PEERS, N_FEAT, PEERS * CAP)
    tile_set = enc_tiles.reshape(PEERS, N_FEAT, BLOCK, PEERS * CAP, BLOCK)
    targets = enc_target.reshape(PEERS, N_FEAT, PEERS * CAP)

    def gather_mesh(packed):
        ids_here, tiles_here, targets_here = packed

        def add_feat(running, per_feat):
            slot_ids, tile_blk, target = per_feat
            blocks = grid_pool[slot_ids].astype(jnp.float32)
            contrib = jnp.einsum('qhs,rqs->qhr', blocks, tile_blk.astype(jnp.float32), precision=lax.Precision.HIGHEST)
            onehot = (target[None, :] == jnp.arange(MB_DEV, dtype=jnp.int32)[:, None]).astype(jnp.float32)
            return running + jnp.einsum('mq,qhr->hmr', onehot, contrib, precision=lax.Precision.HIGHEST), None

        running, _ = lax.scan(add_feat, jnp.zeros((D, MB_DEV, BLOCK), jnp.float32), (ids_here, tiles_here, targets_here))
        return running

    gathered = lax.map(gather_mesh, (grid_ids, tile_set, targets))
    gathered = gathered.transpose(1, 0, 2, 3).reshape(D, NM)
    mesh_new = (mesh_state.astype(jnp.float32) + gathered).astype(jnp.bfloat16)
    mesh_hidden = jax.nn.silu(jnp.dot(mesh_weight.T, mesh_new, preferred_element_type=jnp.float32)).astype(jnp.bfloat16)
    mesh_pool = jnp.concatenate([mesh_hidden.reshape(D, PEERS * MB_DEV, BLOCK).transpose(1, 0, 2), jnp.zeros((1, D, BLOCK), jnp.bfloat16)], 0)
    mesh_ids = jnp.where(send_mesh < MB_DEV, source_idx * MB_DEV + send_mesh, PEERS * MB_DEV).astype(jnp.int32)
    mesh_ids = mesh_ids.transpose(2, 1, 0, 3).reshape(UNITS, PEERS * CAP2)
    pair_ids = jnp.take_along_axis(mesh_ids, dec_slots.reshape(UNITS, GB_DEV * J).astype(jnp.int32), axis=1)

    def decode(packed):
        pair_here, tiles_here, local_cols = packed
        picked = mesh_pool[pair_here].reshape(GB_DEV, J, D, BLOCK).astype(jnp.float32)
        tile_blk = tiles_here.reshape(GB_DEV, BLOCK, J, BLOCK).astype(jnp.float32)
        collected = jnp.einsum('gjhs,grjs->hgr', picked, tile_blk, precision=lax.Precision.HIGHEST)
        collected = collected.reshape(D, GB_DEV * BLOCK).astype(jnp.bfloat16)
        decoded = jax.nn.silu(jnp.dot(dec_first.T, collected, preferred_element_type=jnp.float32)).astype(jnp.bfloat16)
        update = jnp.dot(dec_second.T, decoded, preferred_element_type=jnp.float32)
        return (local_cols.astype(jnp.float32) + update).astype(jnp.bfloat16)

    grid_out = lax.map(decode, (pair_ids, dec_tiles.reshape(UNITS, GB_DEV, BLOCK, J * BLOCK), grid_dev))
    return grid_out.transpose(1, 0, 2).reshape(D, NG)
```

```python
import functools

import jax
import jax.numpy as jnp
from jax import lax
from jax.experimental import pallas as pl
from jax.experimental.pallas import tpu as pltpu
from jax.sharding import PartitionSpec as P

BF = jnp.bfloat16
F32 = jnp.float32
VMEM = pltpu.VMEM
SMEM = pltpu.SMEM
SWAP = [(0, 1), (1, 0)]


def full(space=VMEM):
    return pl.BlockSpec(memory_space=space)


def params(n_dom):
    return pltpu.CompilerParams(vmem_limit_bytes=(12 if n_dom <= 4 else 48) * 1024 * 1024)


def cost(us):
    return pl.CostEstimate(flops=int(us * 4e8), bytes_accessed=int(us * 1e6), transcendentals=0)


def anywhere():
    return pl.BlockSpec(memory_space=pl.ANY)


def silu(x):
    half = 0.5 * x
    return half + half * jnp.tanh(half)


def mm(a, b):
    return jnp.dot(a, b, preferred_element_type=F32)


def turn(v):
    return v.astype(F32).T.astype(BF)


def swap_halves(v, width):
    return jnp.concatenate([v[:, width:], v[:, :width]], axis=1)


def pack_rows(step, blocks, n_dom, at_ref, send_ref, buf, i, outs):
    pair = outs[0].shape[2]
    width = pair // 2
    cols = blocks * width
    here = slice(i * step, (i + 1) * step)
    for p in range(blocks // 2):
        v = buf[0, here, p * pair:(p + 1) * pair]
        buf[1, here, p * pair:(p + 1) * pair] = swap_halves(v, width)
    low = lax.broadcasted_iota(jnp.int32, (step, pair), 1) < width
    for k in range(n_dom):
        for j in range(2):
            peer = lax.rem(at_ref[0] + k, n_dom) * 2 + (at_ref[2] if j == 0 else 1 - at_ref[2])
            vs = []
            for c in range(2):
                b = send_ref[c, peer]
                used = b < blocks
                start = pl.multiple_of(jnp.where(used, b // 2 * pair, cols), pair)
                flip = jnp.where(used & (lax.rem(b, 2) != c), 1, 0)
                vs.append(buf[flip, here, pl.ds(start, pair)])
            outs[k][j, here, :] = jnp.where(low, vs[0], vs[1])


def pack_kernel(blocks, n_dom, at_ref, send_ref, src_ref, *refs):
    outs, buf, sems = refs[:n_dom], refs[n_dom], refs[n_dom + 1]
    rows, cols = src_ref.shape
    parts = 4
    step = rows // parts
    copies = []
    for i in range(parts):
        here = pl.ds(i * step, step)
        copies.append(pltpu.make_async_copy(src_ref.at[here, :], buf.at[0, here, pl.ds(0, cols)], sems.at[i]))
        copies[-1].start()
    buf[0, :, cols:] = jnp.zeros((rows, buf.shape[2] - cols), BF)
    for i in range(parts):
        copies[i].wait()
        pack_rows(step, blocks, n_dom, at_ref, send_ref, buf, i, outs)


def stack_kernel(n_dom, waits, *refs):
    chunks, out = refs[waits:waits + n_dom], refs[waits + n_dom]
    for k in range(n_dom):
        out[k] = chunks[k][1]


def assemble_kernel(sources, at_ref, *refs):
    count = len(sources)
    ws, gots, outs = refs[:count], refs[count:-count], refs[-count:]
    rows = ws[0].shape[0]
    own = pl.multiple_of(at_ref[1] * rows, rows)
    other = pl.multiple_of((1 - at_ref[1]) * rows, rows)
    for i, (which, part) in enumerate(sources):
        outs[i][:, pl.ds(own, rows)] = turn(ws[i][...])
        outs[i][:, pl.ds(other, rows)] = turn(gots[which][part * rows:(part + 1) * rows, :])


def scatter_kernel(n_dom, mesh_blocks, at_ref, tgt_ref, tiles_ref, out_ref):
    block = tiles_ref.shape[0]
    pair = 2 * block
    low = lax.broadcasted_iota(jnp.int32, (1, pair), 1) < block
    for j in range(2):
        for k in range(n_dom):
            sub = at_ref[2] if j == 0 else 1 - at_ref[2]
            peer = lax.rem(at_ref[0] + n_dom - k, n_dom) * 2 + sub
            t = turn(tiles_ref[:, pl.ds(pl.multiple_of(peer * pair, pair), pair)])
            t = jnp.concatenate([t, t], axis=1)
            for c in range(2):
                m = tgt_ref[peer * 2 + c]
                for p in range(mesh_blocks // 2):
                    mask = (jnp.where(low, 2 * p, 2 * p + 1) == m).astype(F32).astype(BF)
                    row = k * pair + c * block
                    out_ref[j, row:row + block, p * pair:(p + 1) * pair] = t[c * block:(c + 1) * block] * mask


def spread_kernel(n_dom, feeding, at_ref, slot_ref, tiles_ref, out_ref):
    g = pl.program_id(0)
    block = tiles_ref.shape[1]
    t = turn(tiles_ref[...].reshape(2 * block, feeding * block))
    low = lax.broadcasted_iota(jnp.int32, (block, 2 * block), 1) < block
    out_ref[...] = jnp.zeros_like(out_ref)
    for h in range(2):
        for i in range(feeding):
            q = slot_ref[i, g * 2 + h]
            peer = q // 2
            k = lax.rem(at_ref[0] + n_dom - peer // 2, n_dom)
            j = jnp.where(lax.rem(peer, 2) == at_ref[2], 0, 1)
            row = pl.multiple_of(((j * n_dom + k) * 2 + lax.rem(q, 2)) * block, block)
            v = t[i * block:(i + 1) * block, :]
            v = jnp.where(low if h == 0 else ~low, v, jnp.zeros_like(v))
            out_ref[pl.ds(row, block), :] += v


def encode_kernel(n_dom, w1t_ref, wide_ref, *rest):
    chunks, out_ref = rest[:n_dom], rest[n_dom]
    x = jnp.concatenate([chunks[k][0] for k in range(n_dom)], axis=1)
    hid = silu(mm(w1t_ref[...], x)).astype(BF)
    out_ref[...] = mm(hid, wide_ref[0])


def gather_kernel(n_dom, at_ref, acc_ref, w1t_ref, w2t_ref, wide_ref, ms_ref, far_ref, g_ref, gb_ref):
    x = jnp.concatenate([far_ref[k] for k in range(n_dom)], axis=1)
    hid = silu(mm(w1t_ref[...], x)).astype(BF)
    acc = acc_ref[...] + mm(hid, wide_ref[1])
    g_ref[...] = mm(w2t_ref[...], acc.astype(BF))
    rows = ms_ref.shape[0]
    here = pl.ds(pl.multiple_of(at_ref[1] * rows, rows), rows)
    g_ref[here, :] += ms_ref[...].astype(F32)
    gb_ref[...] = g_ref[...].astype(BF)


def mesh_kernel(blocks, n_dom, at_ref, send_ref, g_ref, other_ref, mwt_ref, *rest):
    outs, buf = rest[:n_dom], rest[n_dom]
    rows, cols = g_ref.shape
    new = (g_ref[...] + other_ref[...].astype(F32)).astype(BF)
    buf[0, :, :cols] = silu(mm(mwt_ref[...], new)).astype(BF)
    buf[0, :, cols:] = jnp.zeros((rows, buf.shape[2] - cols), BF)
    for i in range(4):
        pack_rows(rows // 4, blocks, n_dom, at_ref, send_ref, buf, i, outs)


def collect_kernel(n_dom, cols, wide_ref, *rest):
    chunks, out_ref = rest[:n_dom], rest[n_dom]
    pool = jnp.concatenate([chunks[k][0] for k in range(n_dom)], axis=1)
    for t in range(out_ref.shape[1] // cols):
        here = slice(t * cols, (t + 1) * cols)
        out_ref[:, here] = mm(pool, wide_ref[:pool.shape[1], here])


def decode_kernel(n_dom, cols, acc_ref, wide_ref, d1t_ref, d2t_ref, grid_ref, far_ref, out_ref, buf, sems):
    pool = jnp.concatenate([far_ref[k] for k in range(n_dom)], axis=1)
    copies = []
    for t in range(grid_ref.shape[1] // cols):
        here = slice(t * cols, (t + 1) * cols)
        got = (acc_ref[:, here] + mm(pool, wide_ref[pool.shape[1]:, here])).astype(BF)
        dec = silu(mm(d1t_ref[...], got)).astype(BF)
        value = (grid_ref[:, here].astype(F32) + mm(d2t_ref[...], dec)).astype(BF)
        if t >= 2:
            copies[t - 2].wait()
        buf[t % 2] = value
        copies.append(pltpu.make_async_copy(buf.at[t % 2], out_ref.at[:, pl.ds(t * cols, cols)], sems.at[t % 2]))
        copies[t].start()
    for copy in copies[-2:]:
        copy.wait()


def move(chunks, n_dom):
    order = sorted(range(1, n_dom), key=lambda k: -min(k, n_dom - k))
    moved = {0: chunks[0]}
    for k in order:
        moved[k] = lax.ppermute(chunks[k], "dom", [(i, (i + k) % n_dom) for i in range(n_dom)])
    return [moved[k] for k in range(n_dom)]


def local(n_dom, n_feat, grid_state, mesh_state, enc_first, enc_second, dec_first, dec_second,
          mesh_weight, send_grid, enc_tiles, enc_target, send_mesh, dec_slots, dec_tiles):
    rows = grid_state.shape[0]
    block = dec_tiles.shape[1]
    grid_cols = grid_state.shape[1]
    grid_blocks = grid_cols // block
    mesh_cols = mesh_state.shape[1]
    mesh_blocks = mesh_cols // block
    slots = enc_target.shape[-1]
    feeding = dec_slots.shape[1]
    pair = 2 * block
    at = jnp.stack([lax.axis_index("dom"), lax.axis_index("feat"), lax.axis_index("sub")]).astype(jnp.int32)
    send_grid = send_grid.reshape(slots // 2, 2).T
    send_mesh = send_mesh.reshape(slots // 2, 2).T
    chunk = jax.ShapeDtypeStruct((2, rows, pair), BF)
    square = jax.ShapeDtypeStruct((rows, rows), BF)
    call = functools.partial(pl.pallas_call, compiler_params=params(n_dom))

    out = call(
        functools.partial(pack_kernel, grid_blocks, n_dom),
        out_shape=[chunk] * n_dom,
        in_specs=[full(SMEM), full(SMEM), anywhere()],
        out_specs=[full()] * n_dom,
        scratch_shapes=[VMEM((2, rows, grid_cols + pair), BF), pltpu.SemaphoreType.DMA((4,))],
        cost_estimate=cost(1),
        name="pack",
    )(at, send_grid, grid_state)
    near = move(out, n_dom)

    def whole(groups):
        ws = [w for group in groups for w in group]
        if n_feat != 2:
            gathered = lax.all_gather(jnp.stack(ws), "feat", axis=1, tiled=True).transpose(0, 2, 1)
            return [gathered[i] for i in range(len(ws))]
        gots = [lax.ppermute(jnp.concatenate(group, axis=0), "feat", SWAP) for group in groups]
        sources = [(i, part) for i, group in enumerate(groups) for part in range(len(group))]
        return call(
            functools.partial(assemble_kernel, sources),
            out_shape=[square] * len(ws),
            in_specs=[full(SMEM)] + [full()] * (len(ws) + len(gots)),
            out_specs=[full()] * len(ws),
            cost_estimate=cost(0),
            name="assemble",
        )(at, *ws, *gots)

    def cross(chunks, *waits):
        mine = call(
            functools.partial(stack_kernel, n_dom, len(waits)),
            out_shape=jax.ShapeDtypeStruct((n_dom, rows, pair), BF),
            in_specs=[anywhere()] * len(waits) + [full()] * n_dom,
            out_specs=full(),
            cost_estimate=cost(0),
            name="stack",
        )(*waits, *chunks)
        return lax.ppermute(mine, "sub", SWAP)

    w1t, w2t, mwt = whole([[enc_first], [enc_second, mesh_weight]])
    to_mesh = call(
        functools.partial(scatter_kernel, n_dom, mesh_blocks),
        out_shape=jax.ShapeDtypeStruct((2, n_dom * pair, mesh_cols), BF),
        in_specs=[full(SMEM), full(SMEM), full()],
        out_specs=full(),
        cost_estimate=cost(0),
        name="scatter",
    )(at, enc_target.reshape(slots), enc_tiles.reshape(block, slots * block))
    to_grid = call(
        functools.partial(spread_kernel, n_dom, feeding),
        grid=(grid_blocks // 2,),
        out_shape=jax.ShapeDtypeStruct((slots * block, grid_cols), BF),
        in_specs=[full(SMEM), full(SMEM), pl.BlockSpec((2, block, feeding * block), lambda i: (i, 0, 0))],
        out_specs=pl.BlockSpec((slots * block, pair), lambda i: (0, i)),
        cost_estimate=cost(0),
        name="spread",
    )(at, dec_slots.T, dec_tiles)

    far = cross(near, w1t, to_mesh, to_grid)
    acc = call(
        functools.partial(encode_kernel, n_dom),
        out_shape=jax.ShapeDtypeStruct((rows, mesh_cols), F32),
        in_specs=[full()] * (2 + n_dom),
        out_specs=full(),
        cost_estimate=cost(0.5),
        name="encode",
    )(w1t, to_mesh, *near)
    g, gb = call(
        functools.partial(gather_kernel, n_dom),
        out_shape=[jax.ShapeDtypeStruct((rows, mesh_cols), F32), jax.ShapeDtypeStruct((rows, mesh_cols), BF)],
        in_specs=[full(SMEM)] + [full()] * 6,
        out_specs=[full()] * 2,
        cost_estimate=cost(0.5),
        name="gather",
    )(at, acc, w1t, w2t, to_mesh, mesh_state, far)
    if n_feat == 2:
        other = lax.ppermute(gb, "feat", SWAP)
    else:
        other = (lax.psum(g, "feat") - g).astype(BF)
    out = call(
        functools.partial(mesh_kernel, mesh_blocks, n_dom),
        out_shape=[chunk] * n_dom,
        in_specs=[full(SMEM), full(SMEM)] + [full()] * 3,
        out_specs=[full()] * n_dom,
        scratch_shapes=[VMEM((2, rows, mesh_cols + pair), BF)],
        cost_estimate=cost(1),
        name="mesh",
    )(at, send_mesh, g, other, mwt)

    near = move(out, n_dom)
    d1t, d2t = whole([[dec_first], [dec_second]])
    far = cross(near, d1t)
    cols = 4 * block
    acc = call(
        functools.partial(collect_kernel, n_dom, cols),
        out_shape=jax.ShapeDtypeStruct((rows, grid_cols), F32),
        in_specs=[full()] * (1 + n_dom),
        out_specs=full(),
        cost_estimate=cost(1),
        name="collect",
    )(to_grid, *near)
    return call(
        functools.partial(decode_kernel, n_dom, cols),
        out_shape=jax.ShapeDtypeStruct(grid_state.shape, BF),
        in_specs=[full()] * 6,
        out_specs=anywhere(),
        scratch_shapes=[VMEM((2, rows, cols), BF), pltpu.SemaphoreType.DMA((2,))],
        cost_estimate=cost(3),
        name="decode",
    )(acc, to_grid, d1t, d2t, grid_state, far)


def solution(mesh):
    whole = ("ens", "dom", "sub", "feat")
    share = ("ens", "dom", "sub")
    in_specs = (
        P(None, whole),
        P("feat", share),
        P("feat", None),
        P("feat", None),
        P("feat", None),
        P("feat", None),
        P("feat", None),
        P(share, "feat", None, None),
        P(share, "feat", None, None),
        P(share, "feat", None),
        P(share, "feat", None, None),
        P(whole, None),
        P(whole, None, None),
    )
    return jax.shard_map(
        functools.partial(local, mesh.shape["dom"], mesh.shape["feat"]),
        mesh=mesh, in_specs=in_specs, out_specs=P(None, whole), check_vma=False,
    )
```

```python
import functools

import jax
import jax.numpy as jnp
from jax import lax
from jax.experimental import pallas as pl
from jax.experimental.pallas import tpu as pltpu
from jax.sharding import PartitionSpec as P

BF = jnp.bfloat16
F32 = jnp.float32
VMEM = pltpu.VMEM
SMEM = pltpu.SMEM
SWAP = [(0, 1), (1, 0)]


def full(space=VMEM):
    return pl.BlockSpec(memory_space=space)


def params(mib):
    return pltpu.CompilerParams(vmem_limit_bytes=int(mib * 1024 * 1024))


def cost(us):
    return pl.CostEstimate(flops=int(us * 4e8), bytes_accessed=int(us * 1e6), transcendentals=0)


def anywhere():
    return pl.BlockSpec(memory_space=pl.ANY)


def outside():
    return pl.BlockSpec(memory_space=pltpu.HBM)


def silu(x):
    half = 0.5 * x
    return half + half * jnp.tanh(half)


def mm(a, b):
    return jnp.dot(a, b, preferred_element_type=F32)


def mt(w, x):
    return lax.dot_general(w, x, (((0,), (0,)), ((), ())), preferred_element_type=F32)


def turn(v):
    return v.astype(F32).T.astype(BF)


def swap_halves(v, width):
    return jnp.concatenate([v[:, width:], v[:, :width]], axis=1)


def pack_rows(step, blocks, n_dom, at_ref, send_ref, buf, i, outs):
    pair = outs[0].shape[2]
    width = pair // 2
    cols = blocks * width
    here = slice(i * step, (i + 1) * step)
    for p in range(blocks // 2):
        v = buf[0, here, p * pair:(p + 1) * pair]
        buf[1, here, p * pair:(p + 1) * pair] = swap_halves(v, width)
    low = lax.broadcasted_iota(jnp.int32, (step, pair), 1) < width
    for k in range(n_dom):
        for j in range(2):
            peer = (at_ref[0] ^ k) * 2 + (at_ref[2] ^ j)
            vs = []
            for c in range(2):
                b = send_ref[c, peer]
                used = b < blocks
                start = pl.multiple_of(jnp.where(used, b // 2 * pair, cols), pair)
                flip = jnp.where(used & (lax.rem(b, 2) != c), 1, 0)
                vs.append(buf[flip, here, pl.ds(start, pair)])
            outs[k][j, here, :] = jnp.where(low, vs[0], vs[1])


def pack_kernel(blocks, n_dom, at_ref, send_ref, src_ref, *refs):
    outs, buf, sems = refs[:n_dom], refs[n_dom], refs[n_dom + 1]
    rows, cols = src_ref.shape
    parts = 4
    step = rows // parts
    copies = []
    for i in range(parts):
        here = pl.ds(i * step, step)
        copies.append(pltpu.make_async_copy(src_ref.at[here, :], buf.at[0, here, pl.ds(0, cols)], sems.at[i]))
        copies[-1].start()
    buf[0, :, cols:] = jnp.zeros((rows, buf.shape[2] - cols), BF)
    for i in range(parts):
        copies[i].wait()
        pack_rows(step, blocks, n_dom, at_ref, send_ref, buf, i, outs)


def stack_kernel(n_dom, waits, *refs):
    chunks, out = refs[waits:waits + n_dom], refs[waits + n_dom]
    for i, k in enumerate(order_of(n_dom)):
        out[k] = chunks[i][1]


def joined(at_ref, refs):
    if len(refs) == 1:
        return refs[0][...]
    own, got = refs[0][...], refs[1][...]
    first = at_ref[1] == 0
    return jnp.concatenate([jnp.where(first, own, got), jnp.where(first, got, own)], axis=0)


def scatter_kernel(n_dom, mesh_blocks, at_ref, tgt_ref, tiles_ref, ms_ref, out_ref, split_ref):
    block = tiles_ref.shape[0]
    pair, part = 2 * block, block // 2
    wide = mesh_blocks * part
    group = lax.broadcasted_iota(jnp.int32, (1, pair), 1) // part
    for j in range(2):
        for k in range(n_dom):
            peer = (at_ref[0] ^ k) * 2 + (at_ref[2] ^ j)
            t = turn(tiles_ref[:, pl.ds(pl.multiple_of(peer * pair, pair), pair)])
            for h in range(2):
                spread = jnp.concatenate([t[:, h * part:(h + 1) * part]] * 4, axis=1)
                for c in range(2):
                    m = tgt_ref[peer * 2 + c]
                    row = k * pair + c * block
                    for p in range(mesh_blocks // 4):
                        mask = (group + 4 * p == m).astype(F32).astype(BF)
                        at = h * wide + p * pair
                        out_ref[j, row:row + block, at:at + pair] = spread[c * block:(c + 1) * block] * mask
    ms = ms_ref[...]
    for h in range(2):
        for p in range(mesh_blocks // 4):
            split_ref[:, h * wide + p * pair:h * wide + (p + 1) * pair] = jnp.concatenate(
                [ms[:, m * block + h * part:m * block + (h + 1) * part] for m in range(4 * p, 4 * p + 4)], axis=1
            )


def spread_kernel(n_dom, feeding, at_ref, slot_ref, tiles_ref, out_ref):
    g = pl.program_id(0)
    block = tiles_ref.shape[1]
    t = turn(tiles_ref[...].reshape(2 * block, feeding * block))
    half = block // 2
    low = lax.broadcasted_iota(jnp.int32, (half, 2 * block), 1) < block
    out_ref[...] = jnp.zeros_like(out_ref)
    for h in range(2):
        for i in range(feeding):
            q = slot_ref[i, g * 2 + h]
            peer = q // 2
            k = at_ref[0] ^ (peer // 2)
            j = at_ref[2] ^ lax.rem(peer, 2)
            for part in range(2):
                row = part * (out_ref.shape[0] // 2) + ((k * 2 + j) * 2 + lax.rem(q, 2)) * half
                v = t[i * block + part * half:i * block + (part + 1) * half, :]
                v = jnp.where(low if h == 0 else ~low, v, jnp.zeros_like(v))
                out_ref[pl.ds(pl.multiple_of(row, half), half), :] += v


def encode_kernel(n_dom, at_ref, wide_ref, *rest):
    chunks, ws, out_ref = rest[:n_dom], rest[n_dom:-1], rest[-1]
    place = order_of(n_dom).index
    x = jnp.concatenate([chunks[place(k)][0] for k in range(n_dom)], axis=1)
    hid = silu(mt(joined(at_ref, ws), x)).astype(BF)
    out_ref[...] = mm(hid, wide_ref[0])


def gather_kernel(n_dom, at_ref, acc_ref, wide_ref, ms_ref, far_ref, *rest):
    ws, (g_ref, first_ref, second_ref) = rest[:-3], rest[-3:]
    count = len(ws) // 2
    x = jnp.concatenate([far_ref[k] for k in range(n_dom)], axis=1)
    hid = silu(mt(joined(at_ref, ws[:count]), x)).astype(BF)
    acc = acc_ref[...] + mm(hid, wide_ref[1])
    g_ref[...] = mt(joined(at_ref, ws[count:]), acc.astype(BF))
    rows = ms_ref.shape[0]
    here = pl.ds(pl.multiple_of(at_ref[1] * rows, rows), rows)
    g_ref[here, :] += ms_ref[...].astype(F32)
    half = g_ref.shape[1] // 2
    first_ref[...] = g_ref[:, :half].astype(BF)
    second_ref[...] = g_ref[:, half:].astype(BF)


def mesh_kernel(blocks, n_dom, h, at_ref, send_ref, g_ref, other_ref, mw_ref, *rest):
    outs, buf = rest[-1 - n_dom:-1], rest[-1]
    rows = g_ref.shape[0]
    cols = g_ref.shape[1] // 2
    new = (g_ref[:, h * cols:(h + 1) * cols] + other_ref[...].astype(F32)).astype(BF)
    hid = silu(mt(mw_ref[...], new)).astype(BF)
    part = cols // blocks
    for p in range(cols // 128):
        v = hid[:, p * 128:(p + 1) * 128]
        buf[0, :, p * 128:(p + 1) * 128] = v
        for turned in range(1, 4):
            cut = 128 - turned * part
            buf[turned, :, p * 128:(p + 1) * 128] = jnp.concatenate([v[:, cut:], v[:, :cut]], axis=1)
    buf[0, :, cols:] = jnp.zeros((rows, 128), BF)
    step = rows // 4
    group = lax.broadcasted_iota(jnp.int32, (step, 128), 1) // part
    for k in range(n_dom):
        picks = []
        for i in range(4):
            b = send_ref[i % 2, (at_ref[0] ^ k) * 2 + (at_ref[2] ^ (i // 2))]
            used = b < blocks
            start = pl.multiple_of(jnp.where(used, b // 4 * 128, cols), 128)
            picks.append((jnp.where(used, lax.rem(i + 4 - lax.rem(b, 4), 4), 0), start))
        for r in range(4):
            here = slice(r * step, (r + 1) * step)
            vs = [buf[turned, here, pl.ds(start, 128)] for turned, start in picks]
            outs[k][here, :] = jnp.where(
                group < 2, jnp.where(group == 0, vs[0], vs[1]), jnp.where(group == 2, vs[2], vs[3])
            )


def first_mesh_kernel(blocks, n_dom, at_ref, send_ref, g_ref, other_ref, mw_ref, later_ref, *rest):
    outs, later_out, buf = rest[:n_dom], rest[n_dom], rest[n_dom + 1]
    mesh_kernel(blocks, n_dom, 0, at_ref, send_ref, g_ref, other_ref, mw_ref, *outs, buf)
    later_out[...] = later_ref[...]


def hold_kernel(ready_ref, x_ref, out_ref):
    out_ref[...] = x_ref[...]


def join_kernel(n_dom, waits, *refs):
    chunks, out = refs[waits:waits + n_dom], refs[waits + n_dom]
    for i, k in enumerate(order_of(n_dom)):
        out[k] = chunks[i][...]


def pool_of(n_dom, near, far_ref):
    place = order_of(n_dom).index
    low = lax.broadcasted_iota(jnp.int32, far_ref.shape[1:], 1) < far_ref.shape[2] // 2
    return jnp.concatenate([jnp.where(low, near[place(k)][...], far_ref[k]) for k in range(n_dom)], axis=1)


def collect_kernel(n_dom, ready_ref, wide_ref, far_ref, *rest):
    chunks, out_ref = rest[:n_dom], rest[n_dom]
    pool = pool_of(n_dom, chunks, far_ref)
    out_ref[...] = mm(pool, wide_ref[:pool.shape[1], :])


def decode_kernel(n_dom, cols, acc_ref, wide_ref, d1_ref, d2_ref, grid_ref, far_ref, *rest):
    chunks, (out_ref, buf, sems) = rest[:n_dom], rest[n_dom:]
    pool = pool_of(n_dom, chunks, far_ref)
    got = (acc_ref[...] + mm(pool, wide_ref[pool.shape[1]:, :])).astype(BF)
    dec = silu(mt(d1_ref[...], got)).astype(BF)
    copies = []
    for t in range(grid_ref.shape[1] // cols):
        here = slice(t * cols, (t + 1) * cols)
        buf[:, here] = (grid_ref[:, here].astype(F32) + mt(d2_ref[...], dec[:, here])).astype(BF)
        copies.append(pltpu.make_async_copy(
            buf.at[:, pl.ds(t * cols, cols)], out_ref.at[:, pl.ds(t * cols, cols)], sems.at[t]
        ))
        copies[t].start()
    for copy in copies:
        copy.wait()


def order_of(n_dom):
    return [0] + list(range(n_dom // 2, n_dom)) + list(range(1, n_dom // 2))


def move(chunks, n_dom):
    moved = {0: chunks[0]}
    for k in order_of(n_dom)[1:]:
        moved[k] = lax.ppermute(chunks[k], "dom", [(i, i ^ k) for i in range(n_dom)])
    return [moved[k] for k in range(n_dom)]


def local(n_dom, n_feat, grid_state, mesh_state, enc_first, enc_second, dec_first, dec_second,
          mesh_weight, send_grid, enc_tiles, enc_target, send_mesh, dec_slots, dec_tiles):
    rows = grid_state.shape[0]
    block = dec_tiles.shape[1]
    grid_cols = grid_state.shape[1]
    grid_blocks = grid_cols // block
    mesh_cols = mesh_state.shape[1]
    mesh_blocks = mesh_cols // block
    slots = enc_target.shape[-1]
    feeding = dec_slots.shape[1]
    pair = 2 * block
    at = jnp.stack([lax.axis_index("dom"), lax.axis_index("feat"), lax.axis_index("sub")]).astype(jnp.int32)
    send_grid = send_grid.reshape(slots // 2, 2).T
    send_mesh = send_mesh.reshape(slots // 2, 2).T
    chunk = jax.ShapeDtypeStruct((2, rows, pair), BF)
    call = functools.partial(pl.pallas_call, compiler_params=params(12 if n_dom <= 4 else 48))

    out = pl.pallas_call(
        functools.partial(pack_kernel, grid_blocks, n_dom),
        out_shape=[chunk] * n_dom,
        in_specs=[full(SMEM), full(SMEM), outside()],
        out_specs=[full()] * n_dom,
        scratch_shapes=[VMEM((2, rows, grid_cols + pair), BF), pltpu.SemaphoreType.DMA((4,))],
        cost_estimate=cost(1),
        compiler_params=params(12),
        name="pack",
    )(at, send_grid, grid_state)
    near = move(out, n_dom)

    def whole(w):
        return lax.all_gather(w, "feat", axis=0, tiled=True)

    def cross(kernel, chunks, *waits):
        mine = call(
            functools.partial(kernel, n_dom, len(waits)),
            out_shape=jax.ShapeDtypeStruct((n_dom, rows, pair), BF),
            in_specs=[anywhere()] * len(waits) + [full()] * n_dom,
            out_specs=full(),
            cost_estimate=cost(0),
            name="stack",
        )(*waits, *[chunks[k] for k in order_of(n_dom)])
        return lax.ppermute(mine, "sub", SWAP)

    def rows_of(w):
        return [w, lax.ppermute(w, "feat", SWAP)] if n_feat == 2 else [whole(w)]

    w1, w2, mw = rows_of(enc_first), rows_of(enc_second), whole(mesh_weight)
    to_mesh, split_state = call(
        functools.partial(scatter_kernel, n_dom, mesh_blocks),
        out_shape=[
            jax.ShapeDtypeStruct((2, n_dom * pair, mesh_cols), BF),
            jax.ShapeDtypeStruct(mesh_state.shape, BF),
        ],
        in_specs=[full(SMEM), full(SMEM), full(), full()],
        out_specs=[full(), full()],
        cost_estimate=cost(0),
        name="scatter",
    )(at, enc_target.reshape(slots), enc_tiles.reshape(block, slots * block), mesh_state)
    to_grid = call(
        functools.partial(spread_kernel, n_dom, feeding),
        grid=(grid_blocks // 2,),
        out_shape=jax.ShapeDtypeStruct((slots * block, grid_cols), BF),
        in_specs=[full(SMEM), full(SMEM), pl.BlockSpec((2, block, feeding * block), lambda i: (i, 0, 0))],
        out_specs=pl.BlockSpec((slots * block, pair), lambda i: (0, i)),
        cost_estimate=cost(0),
        name="spread",
    )(at, dec_slots.T, dec_tiles)

    d1 = whole(dec_first)
    far = cross(stack_kernel, near, w1[-1], w2[-1], mw, d1, to_mesh)
    acc = call(
        functools.partial(encode_kernel, n_dom),
        out_shape=jax.ShapeDtypeStruct((rows, mesh_cols), F32),
        in_specs=[full(SMEM)] + [full()] * (1 + n_dom + len(w1)),
        out_specs=full(),
        cost_estimate=cost(0.5),
        name="encode",
    )(at, to_mesh, *[near[k] for k in order_of(n_dom)], *w1)
    half = jax.ShapeDtypeStruct((rows, mesh_cols // 2), BF)
    g, first, second = call(
        functools.partial(gather_kernel, n_dom),
        out_shape=[jax.ShapeDtypeStruct((rows, mesh_cols), F32), half, half],
        in_specs=[full(SMEM)] + [full()] * (4 + len(w1) + len(w2)),
        out_specs=[full()] * 3,
        cost_estimate=cost(0.5),
        name="gather",
    )(at, acc, to_mesh, split_state, far, *w1, *w2)

    def other_feat(x):
        if n_feat == 2:
            return lax.ppermute(x, "feat", SWAP)
        return (lax.psum(x.astype(F32), "feat") - x.astype(F32)).astype(BF)

    thin = jax.ShapeDtypeStruct((rows, pair), BF)
    scratch = [VMEM((4, rows, mesh_cols // 2 + pair), BF)]
    *out, second = call(
        functools.partial(first_mesh_kernel, mesh_blocks, n_dom),
        out_shape=[thin] * n_dom + [half],
        in_specs=[full(SMEM), full(SMEM)] + [full()] * 4,
        out_specs=[full()] * (n_dom + 1),
        scratch_shapes=scratch,
        cost_estimate=cost(0.5),
        name="mesh",
    )(at, send_mesh, g, other_feat(first), mw, second)
    near_first = move(out, n_dom)
    out = call(
        functools.partial(mesh_kernel, mesh_blocks, n_dom, 1),
        out_shape=[thin] * n_dom,
        in_specs=[full(SMEM), full(SMEM)] + [full()] * 3,
        out_specs=[full()] * n_dom,
        scratch_shapes=scratch,
        cost_estimate=cost(0.5),
        name="mesh",
    )(at, send_mesh, g, other_feat(second), mw)
    near_second = move(out, n_dom)
    d2 = whole(call(
        hold_kernel,
        out_shape=jax.ShapeDtypeStruct(dec_second.shape, BF),
        in_specs=[anywhere(), full()],
        out_specs=full(),
        cost_estimate=cost(0),
        name="hold",
    )(out[0], dec_second))
    ordered = order_of(n_dom)
    far_first = cross(join_kernel, near_first, to_grid, out[0], d2)
    far_second = cross(join_kernel, near_second)
    acc = call(
        functools.partial(collect_kernel, n_dom),
        out_shape=jax.ShapeDtypeStruct((rows, grid_cols), F32),
        in_specs=[anywhere()] + [full()] * (2 + n_dom),
        out_specs=full(),
        cost_estimate=cost(0.5),
        name="collect",
    )(near_second[ordered[-1]], to_grid, far_first, *[near_first[k] for k in ordered])
    return call(
        functools.partial(decode_kernel, n_dom, grid_cols // 2),
        out_shape=jax.ShapeDtypeStruct(grid_state.shape, BF),
        in_specs=[full()] * (6 + n_dom),
        out_specs=anywhere(),
        scratch_shapes=[VMEM((rows, grid_cols), BF), pltpu.SemaphoreType.DMA((2,))],
        cost_estimate=cost(3),
        name="decode",
    )(acc, to_grid, d1, d2, grid_state, far_second, *[near_second[k] for k in ordered])


def solution(mesh):
    whole = ("ens", "dom", "sub", "feat")
    share = ("ens", "dom", "sub")
    in_specs = (
        P(None, whole),
        P("feat", share),
        P("feat", None),
        P("feat", None),
        P("feat", None),
        P("feat", None),
        P("feat", None),
        P(share, "feat", None, None),
        P(share, "feat", None, None),
        P(share, "feat", None),
        P(share, "feat", None, None),
        P(whole, None),
        P(whole, None, None),
    )
    return jax.shard_map(
        functools.partial(local, mesh.shape["dom"], mesh.shape["feat"]),
        mesh=mesh, in_specs=in_specs, out_specs=P(None, whole), check_vma=False,
    )
```

```python
import functools

import jax
import jax.numpy as jnp
from jax import lax
from jax.experimental import pallas as pl
from jax.experimental.pallas import tpu as pltpu
from jax.sharding import PartitionSpec as P

BF = jnp.bfloat16
F32 = jnp.float32
VMEM = pltpu.VMEM
SMEM = pltpu.SMEM
SWAP = [(0, 1), (1, 0)]


def full(space=VMEM):
    return pl.BlockSpec(memory_space=space)


def params(mib):
    return pltpu.CompilerParams(vmem_limit_bytes=int(mib * 1024 * 1024))


def cost(us):
    return pl.CostEstimate(flops=int(us * 4e8), bytes_accessed=int(us * 1e6), transcendentals=0)


def anywhere():
    return pl.BlockSpec(memory_space=pl.ANY)


def silu(x):
    half = 0.5 * x
    return half + half * jnp.tanh(half)


def mm(a, b):
    return jnp.dot(a, b, preferred_element_type=F32)


def mt(w, x):
    return lax.dot_general(w, x, (((0,), (0,)), ((), ())), preferred_element_type=F32)


def turn(v):
    return v.astype(F32).T.astype(BF)


def swap_halves(v, width):
    return jnp.concatenate([v[:, width:], v[:, :width]], axis=1)


def pack_rows(step, blocks, n_dom, at_ref, send_ref, src_ref, buf, i, outs):
    pair = outs[0].shape[2]
    width = pair // 2
    cols = blocks * width
    here = slice(i * step, (i + 1) * step)
    for p in range(blocks // 2):
        v = src_ref[here, p * pair:(p + 1) * pair]
        buf[0, here, p * pair:(p + 1) * pair] = v
        buf[1, here, p * pair:(p + 1) * pair] = swap_halves(v, width)
    low = lax.broadcasted_iota(jnp.int32, (step, pair), 1) < width
    for k in range(n_dom):
        for j in range(2):
            peer = (at_ref[0] ^ k) * 2 + (at_ref[2] ^ j)
            vs = []
            for c in range(2):
                b = send_ref[c, peer]
                used = b < blocks
                start = pl.multiple_of(jnp.where(used, b // 2 * pair, cols), pair)
                flip = jnp.where(used & (lax.rem(b, 2) != c), 1, 0)
                vs.append(buf[flip, here, pl.ds(start, pair)])
            outs[k][j, here, :] = jnp.where(low, vs[0], vs[1])


def pack_kernel(blocks, n_dom, at_ref, send_ref, src_ref, *refs):
    outs, buf = refs[:n_dom], refs[n_dom]
    rows, cols = src_ref.shape
    buf[0, :, cols:] = jnp.zeros((rows, buf.shape[2] - cols), BF)
    for i in range(4):
        pack_rows(rows // 4, blocks, n_dom, at_ref, send_ref, src_ref, buf, i, outs)


def stack_kernel(n_dom, waits, *refs):
    chunks, out = refs[:n_dom], refs[n_dom + waits]
    for i, k in enumerate(order_of(n_dom)):
        out[k] = chunks[i][1]


def joined(at_ref, refs):
    if len(refs) == 1:
        return refs[0][...]
    own, got = refs[0][...], refs[1][...]
    first = at_ref[1] == 0
    return jnp.concatenate([jnp.where(first, own, got), jnp.where(first, got, own)], axis=0)


def scatter_kernel(n_dom, mesh_blocks, at_ref, tgt_ref, tiles_ref, ms_ref, out_ref, split_ref):
    block = tiles_ref.shape[0]
    pair, part = 2 * block, block // 2
    wide = mesh_blocks * part
    group = lax.broadcasted_iota(jnp.int32, (1, pair), 1) // part
    for j in range(2):
        for k in range(n_dom):
            peer = (at_ref[0] ^ k) * 2 + (at_ref[2] ^ j)
            t = turn(tiles_ref[:, pl.ds(pl.multiple_of(peer * pair, pair), pair)])
            for h in range(2):
                spread = jnp.concatenate([t[:, h * part:(h + 1) * part]] * 4, axis=1)
                for c in range(2):
                    m = tgt_ref[peer * 2 + c]
                    row = k * pair + c * block
                    for p in range(mesh_blocks // 4):
                        mask = (group + 4 * p == m).astype(F32).astype(BF)
                        at = h * wide + p * pair
                        out_ref[j, row:row + block, at:at + pair] = spread[c * block:(c + 1) * block] * mask
    ms = ms_ref[...]
    for h in range(2):
        for p in range(mesh_blocks // 4):
            split_ref[:, h * wide + p * pair:h * wide + (p + 1) * pair] = jnp.concatenate(
                [ms[:, m * block + h * part:m * block + (h + 1) * part] for m in range(4 * p, 4 * p + 4)], axis=1
            )


def spread_kernel(n_dom, feeding, at_ref, slot_ref, tiles_ref, out_ref):
    g = pl.program_id(0)
    block = tiles_ref.shape[1]
    t = turn(tiles_ref[...].reshape(2 * block, feeding * block))
    half = block // 2
    low = lax.broadcasted_iota(jnp.int32, (half, 2 * block), 1) < block
    out_ref[...] = jnp.zeros_like(out_ref)
    for h in range(2):
        for i in range(feeding):
            q = slot_ref[i, g * 2 + h]
            peer = q // 2
            k = at_ref[0] ^ (peer // 2)
            j = at_ref[2] ^ lax.rem(peer, 2)
            for part in range(2):
                row = part * (out_ref.shape[0] // 2) + ((j * n_dom + k) * 2 + lax.rem(q, 2)) * half
                v = t[i * block + part * half:i * block + (part + 1) * half, :]
                v = jnp.where(low if h == 0 else ~low, v, jnp.zeros_like(v))
                out_ref[pl.ds(pl.multiple_of(row, half), half), :] += v


def encode_kernel(n_dom, at_ref, wide_ref, *rest):
    chunks, ws, out_ref = rest[:n_dom], rest[n_dom:-1], rest[-1]
    place = order_of(n_dom).index
    x = jnp.concatenate([chunks[place(k)][0] for k in range(n_dom)], axis=1)
    hid = silu(mt(joined(at_ref, ws), x)).astype(BF)
    out_ref[...] = mm(hid, wide_ref[0])


def messages(at_ref, ws, h, total, ms_ref, g_ref, out_ref):
    g_ref[...] = mt(joined(at_ref, ws), total)
    rows = ms_ref.shape[0]
    cols = g_ref.shape[1]
    here = pl.ds(pl.multiple_of(at_ref[1] * rows, rows), rows)
    g_ref[here, :] += ms_ref[:, h * cols:(h + 1) * cols].astype(F32)
    out_ref[...] = g_ref[...].astype(BF)


def gather_kernel(n_dom, at_ref, acc_ref, wide_ref, ms_ref, far_ref, *rest):
    ws, (g_ref, first_ref, later_ref) = rest[:-3], rest[-3:]
    count = len(ws) // 2
    half = g_ref.shape[1]
    x = jnp.concatenate([far_ref[k] for k in range(n_dom)], axis=1)
    hid = silu(mt(joined(at_ref, ws[:count]), x)).astype(BF)
    total = (acc_ref[...] + mm(hid, wide_ref[1])).astype(BF)
    messages(at_ref, ws[count:], 0, total[:, :half], ms_ref, g_ref, first_ref)
    later_ref[...] = total[:, half:]


def later_kernel(at_ref, total_ref, ms_ref, *rest):
    ws, (g_ref, out_ref) = rest[:-2], rest[-2:]
    messages(at_ref, ws, 1, total_ref[...], ms_ref, g_ref, out_ref)


def mesh_kernel(blocks, n_dom, at_ref, send_ref, g_ref, other_ref, mw_ref, d1_ref, *rest):
    outs, buf = rest[-1 - n_dom:-1], rest[-1]
    rows = g_ref.shape[0]
    cols = g_ref.shape[1]
    new = (g_ref[...] + other_ref[...].astype(F32)).astype(BF)
    hid = silu(mt(mw_ref[...], new)).astype(BF)
    hid = mt(d1_ref[...], hid).astype(BF)
    part = cols // blocks
    for p in range(cols // 128):
        v = hid[:, p * 128:(p + 1) * 128]
        buf[0, :, p * 128:(p + 1) * 128] = v
        for turned in range(1, 4):
            cut = 128 - turned * part
            buf[turned, :, p * 128:(p + 1) * 128] = jnp.concatenate([v[:, cut:], v[:, :cut]], axis=1)
    buf[0, :, cols:] = jnp.zeros((rows, 128), BF)
    step = rows // 4
    group = lax.broadcasted_iota(jnp.int32, (step, 128), 1) // part
    for k in range(n_dom):
        picks = []
        for i in range(4):
            b = send_ref[i % 2, (at_ref[0] ^ k) * 2 + (at_ref[2] ^ (i // 2))]
            used = b < blocks
            start = pl.multiple_of(jnp.where(used, b // 4 * 128, cols), 128)
            picks.append((jnp.where(used, lax.rem(i + 4 - lax.rem(b, 4), 4), 0), start))
        for r in range(4):
            here = slice(r * step, (r + 1) * step)
            vs = [buf[turned, here, pl.ds(start, 128)] for turned, start in picks]
            outs[k][here, :] = jnp.where(
                group < 2, jnp.where(group == 0, vs[0], vs[1]), jnp.where(group == 2, vs[2], vs[3])
            )


def first_mesh_kernel(blocks, n_dom, at_ref, send_ref, g_ref, other_ref, mw_ref, d1_ref, later_ref, ready_ref, *rest):
    outs, later_out, buf = rest[:n_dom], rest[n_dom], rest[n_dom + 1]
    mesh_kernel(blocks, n_dom, at_ref, send_ref, g_ref, other_ref, mw_ref, d1_ref, *outs, buf)
    later_out[...] = later_ref[...]


def hold_kernel(ready_ref, x_ref, out_ref):
    out_ref[...] = x_ref[...]


def paired(chunks, upper):
    width = chunks[0].shape[1] // 2
    low = lax.broadcasted_iota(jnp.int32, chunks[0].shape, 1) < width
    out = []
    for a, b in zip(chunks[::2], chunks[1::2]):
        a, b = (swap_halves(a, width), b) if upper else (a, swap_halves(b, width))
        out.append(jnp.where(low, a, b))
    return out


def join_kernel(n_dom, waits, *refs):
    chunks, out = refs[:n_dom], refs[n_dom + waits]
    place = order_of(n_dom).index
    for i, v in enumerate(paired([chunks[place(k)][...] for k in range(n_dom)], True)):
        out[i] = v


def collect_kernel(n_dom, ready_ref, wide_ref, far_ref, *rest):
    firsts, seconds, out_ref = rest[:n_dom], rest[n_dom:-1], rest[-1]
    place = order_of(n_dom).index
    pool = paired([firsts[place(k)][...] for k in range(n_dom)], False)
    pool += [far_ref[i] for i in range(n_dom // 2)]
    pool += paired([seconds[place(k)][...] for k in range(n_dom)], False)
    pool = jnp.concatenate(pool, axis=1)
    out_ref[...] = mm(pool, wide_ref[:pool.shape[1], :])


def decode_kernel(n_dom, cols, acc_ref, wide_ref, d2_ref, grid_ref, far_ref, out_ref, buf, sems):
    pool = jnp.concatenate([far_ref[i] for i in range(n_dom // 2)], axis=1)
    dec = silu(acc_ref[...] + mm(pool, wide_ref[wide_ref.shape[0] - pool.shape[1]:, :])).astype(BF)
    copies = []
    for t in range(grid_ref.shape[1] // cols):
        here = slice(t * cols, (t + 1) * cols)
        buf[:, here] = (grid_ref[:, here].astype(F32) + mt(d2_ref[...], dec[:, here])).astype(BF)
        copies.append(pltpu.make_async_copy(
            buf.at[:, pl.ds(t * cols, cols)], out_ref.at[:, pl.ds(t * cols, cols)], sems.at[t]
        ))
        copies[t].start()
    for copy in copies:
        copy.wait()


def order_of(n_dom):
    return [0] + list(range(n_dom // 2, n_dom)) + list(range(1, n_dom // 2))


def move(chunks, n_dom):
    moved = {0: chunks[0]}
    for k in order_of(n_dom)[1:]:
        moved[k] = lax.ppermute(chunks[k], "dom", [(i, i ^ k) for i in range(n_dom)])
    return [moved[k] for k in range(n_dom)]


def local(n_dom, n_feat, grid_state, mesh_state, enc_first, enc_second, dec_first, dec_second,
          mesh_weight, send_grid, enc_tiles, enc_target, send_mesh, dec_slots, dec_tiles):
    rows = grid_state.shape[0]
    block = dec_tiles.shape[1]
    grid_cols = grid_state.shape[1]
    grid_blocks = grid_cols // block
    mesh_cols = mesh_state.shape[1]
    mesh_blocks = mesh_cols // block
    slots = enc_target.shape[-1]
    feeding = dec_slots.shape[1]
    pair = 2 * block
    at = jnp.stack([lax.axis_index("dom"), lax.axis_index("feat"), lax.axis_index("sub")]).astype(jnp.int32)
    send_grid = send_grid.reshape(slots // 2, 2).T
    send_mesh = send_mesh.reshape(slots // 2, 2).T
    chunk = jax.ShapeDtypeStruct((2, rows, pair), BF)
    call = functools.partial(pl.pallas_call, compiler_params=params(12 if n_dom <= 4 else 48))

    out = pl.pallas_call(
        functools.partial(pack_kernel, grid_blocks, n_dom),
        out_shape=[chunk] * n_dom,
        in_specs=[full(SMEM), full(SMEM), full()],
        out_specs=[full()] * n_dom,
        scratch_shapes=[VMEM((2, rows, grid_cols + pair), BF)],
        cost_estimate=cost(1),
        compiler_params=params(12),
        name="pack",
    )(at, send_grid, grid_state)
    near = move(out, n_dom)

    def whole(w):
        return lax.all_gather(w, "feat", axis=0, tiled=True)

    def cross(kernel, count, chunks, *waits):
        mine = call(
            functools.partial(kernel, n_dom, len(waits)),
            out_shape=jax.ShapeDtypeStruct((count, rows, pair), BF),
            in_specs=[full()] * n_dom + [anywhere()] * len(waits),
            out_specs=full(),
            cost_estimate=cost(0),
            name="stack",
        )(*[chunks[k] for k in order_of(n_dom)], *waits)
        return lax.ppermute(mine, "sub", SWAP), mine

    def rows_of(w):
        return [w, lax.ppermute(w, "feat", SWAP)] if n_feat == 2 else [whole(w)]

    w1, w2, mw = rows_of(enc_first), rows_of(enc_second), whole(mesh_weight)
    to_mesh, split_state = call(
        functools.partial(scatter_kernel, n_dom, mesh_blocks),
        out_shape=[
            jax.ShapeDtypeStruct((2, n_dom * pair, mesh_cols), BF),
            jax.ShapeDtypeStruct(mesh_state.shape, BF),
        ],
        in_specs=[full(SMEM), full(SMEM), full(), full()],
        out_specs=[full(), full()],
        cost_estimate=cost(0),
        name="scatter",
    )(at, enc_target.reshape(slots), enc_tiles.reshape(block, slots * block), mesh_state)
    to_grid = call(
        functools.partial(spread_kernel, n_dom, feeding),
        grid=(grid_blocks // 2,),
        out_shape=jax.ShapeDtypeStruct((slots * block, grid_cols), BF),
        in_specs=[full(SMEM), full(SMEM), pl.BlockSpec((2, block, feeding * block), lambda i: (i, 0, 0))],
        out_specs=pl.BlockSpec((slots * block, pair), lambda i: (0, i)),
        cost_estimate=cost(0),
        name="spread",
    )(at, dec_slots.T, dec_tiles)

    d1 = whole(dec_first)
    far, _ = cross(stack_kernel, n_dom, near, w1[-1], w2[-1], mw, d1, to_mesh)
    acc = call(
        functools.partial(encode_kernel, n_dom),
        out_shape=jax.ShapeDtypeStruct((rows, mesh_cols), F32),
        in_specs=[full(SMEM)] + [full()] * (1 + n_dom + len(w1)),
        out_specs=full(),
        cost_estimate=cost(0.5),
        name="encode",
    )(at, to_mesh, *[near[k] for k in order_of(n_dom)], *w1)
    half = jax.ShapeDtypeStruct((rows, mesh_cols // 2), BF)
    sums = jax.ShapeDtypeStruct((rows, mesh_cols // 2), F32)
    g_first, first, later = call(
        functools.partial(gather_kernel, n_dom),
        out_shape=[sums, half, half],
        in_specs=[full(SMEM)] + [full()] * (4 + len(w1) + len(w2)),
        out_specs=[full()] * 3,
        cost_estimate=cost(0.5),
        name="gather",
    )(at, acc, to_mesh, split_state, far, *w1, *w2)
    g_second, second = call(
        later_kernel,
        out_shape=[sums, half],
        in_specs=[full(SMEM)] + [full()] * (2 + len(w2)),
        out_specs=[full()] * 2,
        cost_estimate=cost(0.5),
        name="later",
    )(at, later, split_state, *w2)

    def other_feat(x):
        if n_feat == 2:
            return lax.ppermute(x, "feat", SWAP)
        return (lax.psum(x.astype(F32), "feat") - x.astype(F32)).astype(BF)

    thin = jax.ShapeDtypeStruct((rows, pair), BF)
    scratch = [VMEM((4, rows, mesh_cols // 2 + pair), BF)]
    *out, second = call(
        functools.partial(first_mesh_kernel, mesh_blocks, n_dom),
        out_shape=[thin] * n_dom + [half],
        in_specs=[full(SMEM), full(SMEM)] + [full()] * 5 + [anywhere()],
        out_specs=[full()] * (n_dom + 1),
        scratch_shapes=scratch,
        cost_estimate=cost(0.5),
        name="mesh",
    )(at, send_mesh, g_first, other_feat(first), mw, d1, second, to_grid)
    near_first = move(out, n_dom)
    out = call(
        functools.partial(mesh_kernel, mesh_blocks, n_dom),
        out_shape=[thin] * n_dom,
        in_specs=[full(SMEM), full(SMEM)] + [full()] * 4,
        out_specs=[full()] * n_dom,
        scratch_shapes=scratch,
        cost_estimate=cost(0.5),
        name="mesh",
    )(at, send_mesh, g_second, other_feat(second), mw, d1)
    near_second = move(out, n_dom)
    d2 = whole(call(
        hold_kernel,
        out_shape=jax.ShapeDtypeStruct(dec_second.shape, BF),
        in_specs=[anywhere(), full()],
        out_specs=full(),
        cost_estimate=cost(0),
        name="hold",
    )(out[0], dec_second))
    ordered = order_of(n_dom)
    far_first, _ = cross(join_kernel, n_dom // 2, near_first, out[0], d2)
    far_second, ready = cross(join_kernel, n_dom // 2, near_second)
    acc = call(
        functools.partial(collect_kernel, n_dom),
        out_shape=jax.ShapeDtypeStruct((rows, grid_cols), F32),
        in_specs=[anywhere()] + [full()] * (2 + 2 * n_dom),
        out_specs=full(),
        cost_estimate=cost(0.5),
        name="collect",
    )(ready, to_grid, far_first, *[near_first[k] for k in ordered], *[near_second[k] for k in ordered])
    return call(
        functools.partial(decode_kernel, n_dom, grid_cols // 3),
        out_shape=jax.ShapeDtypeStruct(grid_state.shape, BF),
        in_specs=[full()] * 5,
        out_specs=anywhere(),
        scratch_shapes=[VMEM((rows, grid_cols), BF), pltpu.SemaphoreType.DMA((3,))],
        cost_estimate=cost(3),
        name="decode",
    )(acc, to_grid, d2, grid_state, far_second)


def solution(mesh):
    whole = ("ens", "dom", "sub", "feat")
    share = ("ens", "dom", "sub")
    in_specs = (
        P(None, whole),
        P("feat", share),
        P("feat", None),
        P("feat", None),
        P("feat", None),
        P("feat", None),
        P("feat", None),
        P(share, "feat", None, None),
        P(share, "feat", None, None),
        P(share, "feat", None),
        P(share, "feat", None, None),
        P(whole, None),
        P(whole, None, None),
    )
    return jax.shard_map(
        functools.partial(local, mesh.shape["dom"], mesh.shape["feat"]),
        mesh=mesh, in_specs=in_specs, out_specs=P(None, whole), check_vma=False,
    )
```

```python
import functools

import jax
import jax.numpy as jnp
from jax import lax
from jax.experimental import pallas as pl
from jax.experimental.pallas import tpu as pltpu
from jax.sharding import PartitionSpec as P

BF = jnp.bfloat16
F32 = jnp.float32
VMEM = pltpu.VMEM
SMEM = pltpu.SMEM
SWAP = [(0, 1), (1, 0)]


def full(space=VMEM):
    return pl.BlockSpec(memory_space=space)


def params(mib):
    return pltpu.CompilerParams(vmem_limit_bytes=int(mib * 1024 * 1024))


def cost(us):
    return pl.CostEstimate(flops=int(us * 4e8), bytes_accessed=int(us * 1e6), transcendentals=0)


def anywhere():
    return pl.BlockSpec(memory_space=pl.ANY)


def silu(x):
    half = 0.5 * x
    return half + half * jnp.tanh(half)


def mm(a, b):
    return jnp.dot(a, b, preferred_element_type=F32)


def mt(w, x):
    return lax.dot_general(w, x, (((0,), (0,)), ((), ())), preferred_element_type=F32)


def turn(v):
    return v.astype(F32).T.astype(BF)


def swap_halves(v, width):
    return jnp.concatenate([v[:, width:], v[:, :width]], axis=1)


def pack_rows(step, blocks, n_dom, at_ref, send_ref, src_ref, buf, i, outs):
    pair = outs[0].shape[2]
    width = pair // 2
    cols = blocks * width
    here = slice(i * step, (i + 1) * step)
    for p in range(blocks // 2):
        v = src_ref[here, p * pair:(p + 1) * pair]
        buf[0, here, p * pair:(p + 1) * pair] = v
        buf[1, here, p * pair:(p + 1) * pair] = swap_halves(v, width)
    low = lax.broadcasted_iota(jnp.int32, (step, pair), 1) < width
    for k in range(n_dom):
        for j in range(2):
            peer = (at_ref[0] ^ k) * 2 + (at_ref[2] ^ j)
            vs = []
            for c in range(2):
                b = send_ref[c, peer]
                used = b < blocks
                start = pl.multiple_of(jnp.where(used, b // 2 * pair, cols), pair)
                flip = jnp.where(used & (lax.rem(b, 2) != c), 1, 0)
                vs.append(buf[flip, here, pl.ds(start, pair)])
            outs[k][j, here, :] = jnp.where(low, vs[0], vs[1])


def pack_kernel(blocks, n_dom, at_ref, send_ref, src_ref, *refs):
    outs, src, buf, sems = refs[:n_dom], refs[n_dom], refs[n_dom + 1], refs[n_dom + 2]
    rows, cols = src_ref.shape
    parts = 4
    step = rows // parts
    copies = []
    for i in range(parts):
        here = pl.ds(i * step, step)
        copies.append(pltpu.make_async_copy(src_ref.at[here, :], src.at[here, :], sems.at[i]))
        copies[i].start()
    buf[0, :, cols:] = jnp.zeros((rows, buf.shape[2] - cols), BF)
    for i in range(parts):
        copies[i].wait()
        pack_rows(step, blocks, n_dom, at_ref, send_ref, src, buf, i, outs)


def stack_kernel(n_dom, waits, *refs):
    chunks, out = refs[:n_dom], refs[n_dom + waits]
    for i, k in enumerate(order_of(n_dom)):
        out[k] = chunks[i][1]


def joined(at_ref, refs):
    if len(refs) == 1:
        return refs[0][...]
    own, got = refs[0][...], refs[1][...]
    first = at_ref[1] == 0
    return jnp.concatenate([jnp.where(first, own, got), jnp.where(first, got, own)], axis=0)


def scatter_kernel(n_dom, mesh_blocks, at_ref, tgt_ref, tiles_ref, ms_ref, out_ref, split_ref):
    block = tiles_ref.shape[0]
    pair, part = 2 * block, block // 2
    wide = mesh_blocks * part
    group = lax.broadcasted_iota(jnp.int32, (1, pair), 1) // part
    for j in range(2):
        for k in range(n_dom):
            peer = (at_ref[0] ^ k) * 2 + (at_ref[2] ^ j)
            t = turn(tiles_ref[:, pl.ds(pl.multiple_of(peer * pair, pair), pair)])
            for h in range(2):
                spread = jnp.concatenate([t[:, h * part:(h + 1) * part]] * 4, axis=1)
                for c in range(2):
                    m = tgt_ref[peer * 2 + c]
                    row = k * pair + c * block
                    for p in range(mesh_blocks // 4):
                        mask = (group + 4 * p == m).astype(F32).astype(BF)
                        at = h * wide + p * pair
                        out_ref[j, row:row + block, at:at + pair] = spread[c * block:(c + 1) * block] * mask
    ms = ms_ref[...]
    for h in range(2):
        for p in range(mesh_blocks // 4):
            split_ref[:, h * wide + p * pair:h * wide + (p + 1) * pair] = jnp.concatenate(
                [ms[:, m * block + h * part:m * block + (h + 1) * part] for m in range(4 * p, 4 * p + 4)], axis=1
            )


def spread_kernel(n_dom, feeding, at_ref, slot_ref, tiles_ref, out_ref):
    g = pl.program_id(0)
    block = tiles_ref.shape[1]
    t = turn(tiles_ref[...].reshape(2 * block, feeding * block))
    half = block // 2
    low = lax.broadcasted_iota(jnp.int32, (half, 2 * block), 1) < block
    out_ref[...] = jnp.zeros_like(out_ref)
    for h in range(2):
        for i in range(feeding):
            q = slot_ref[i, g * 2 + h]
            peer = q // 2
            k = at_ref[0] ^ (peer // 2)
            j = at_ref[2] ^ lax.rem(peer, 2)
            for part in range(2):
                row = part * (out_ref.shape[0] // 2) + ((j * n_dom + k) * 2 + lax.rem(q, 2)) * half
                v = t[i * block + part * half:i * block + (part + 1) * half, :]
                v = jnp.where(low if h == 0 else ~low, v, jnp.zeros_like(v))
                out_ref[pl.ds(pl.multiple_of(row, half), half), :] += v


def encode_kernel(n_dom, at_ref, wide_ref, *rest):
    chunks, ws, out_ref = rest[:n_dom], rest[n_dom:-1], rest[-1]
    place = order_of(n_dom).index
    x = jnp.concatenate([chunks[place(k)][0] for k in range(n_dom)], axis=1)
    hid = silu(mt(joined(at_ref, ws), x)).astype(BF)
    out_ref[...] = mm(hid, wide_ref[0])


def messages(at_ref, ws, h, total, ms_ref, g_ref, out_ref):
    g_ref[...] = mt(joined(at_ref, ws), total)
    rows = ms_ref.shape[0]
    cols = g_ref.shape[1]
    here = pl.ds(pl.multiple_of(at_ref[1] * rows, rows), rows)
    g_ref[here, :] += ms_ref[:, h * cols:(h + 1) * cols].astype(F32)
    out_ref[...] = g_ref[...].astype(BF)


def gather_kernel(n_dom, at_ref, acc_ref, wide_ref, ms_ref, far_ref, *rest):
    ws, (g_ref, first_ref, later_ref) = rest[:-3], rest[-3:]
    count = len(ws) // 2
    half = g_ref.shape[1]
    x = jnp.concatenate([far_ref[k] for k in range(n_dom)], axis=1)
    hid = silu(mt(joined(at_ref, ws[:count]), x)).astype(BF)
    total = (acc_ref[...] + mm(hid, wide_ref[1])).astype(BF)
    messages(at_ref, ws[count:], 0, total[:, :half], ms_ref, g_ref, first_ref)
    later_ref[...] = total[:, half:]


def later_kernel(at_ref, total_ref, ms_ref, *rest):
    ws, (g_ref, out_ref) = rest[:-2], rest[-2:]
    messages(at_ref, ws, 1, total_ref[...], ms_ref, g_ref, out_ref)


def mesh_kernel(blocks, n_dom, at_ref, send_ref, g_ref, other_ref, mw_ref, d1_ref, *rest):
    outs, buf = rest[-1 - n_dom:-1], rest[-1]
    rows = g_ref.shape[0]
    cols = g_ref.shape[1]
    new = (g_ref[...] + other_ref[...].astype(F32)).astype(BF)
    hid = silu(mt(mw_ref[...], new)).astype(BF)
    hid = mt(d1_ref[...], hid).astype(BF)
    part = cols // blocks
    for p in range(cols // 128):
        v = hid[:, p * 128:(p + 1) * 128]
        buf[0, :, p * 128:(p + 1) * 128] = v
        for turned in range(1, 4):
            cut = 128 - turned * part
            buf[turned, :, p * 128:(p + 1) * 128] = jnp.concatenate([v[:, cut:], v[:, :cut]], axis=1)
    buf[0, :, cols:] = jnp.zeros((rows, 128), BF)
    step = rows // 4
    group = lax.broadcasted_iota(jnp.int32, (step, 128), 1) // part
    for k in range(n_dom):
        picks = []
        for i in range(4):
            b = send_ref[i % 2, (at_ref[0] ^ k) * 2 + (at_ref[2] ^ (i // 2))]
            used = b < blocks
            start = pl.multiple_of(jnp.where(used, b // 4 * 128, cols), 128)
            picks.append((jnp.where(used, lax.rem(i + 4 - lax.rem(b, 4), 4), 0), start))
        for r in range(4):
            here = slice(r * step, (r + 1) * step)
            vs = [buf[turned, here, pl.ds(start, 128)] for turned, start in picks]
            outs[k][here, :] = jnp.where(
                group < 2, jnp.where(group == 0, vs[0], vs[1]), jnp.where(group == 2, vs[2], vs[3])
            )


def first_mesh_kernel(blocks, n_dom, at_ref, send_ref, g_ref, other_ref, mw_ref, d1_ref, later_ref, ready_ref, *rest):
    outs, later_out, buf = rest[:n_dom], rest[n_dom], rest[n_dom + 1]
    mesh_kernel(blocks, n_dom, at_ref, send_ref, g_ref, other_ref, mw_ref, d1_ref, *outs, buf)
    later_out[...] = later_ref[...]


def hold_kernel(ready_ref, x_ref, out_ref):
    out_ref[...] = x_ref[...]


def paired(chunks, upper):
    width = chunks[0].shape[1] // 2
    low = lax.broadcasted_iota(jnp.int32, chunks[0].shape, 1) < width
    out = []
    for a, b in zip(chunks[::2], chunks[1::2]):
        a, b = (swap_halves(a, width), b) if upper else (a, swap_halves(b, width))
        out.append(jnp.where(low, a, b))
    return out


def join_kernel(n_dom, waits, *refs):
    chunks, out = refs[:n_dom], refs[n_dom + waits]
    place = order_of(n_dom).index
    for i, v in enumerate(paired([chunks[place(k)][...] for k in range(n_dom)], True)):
        out[i] = v


def collect_kernel(n_dom, ready_ref, wide_ref, far_ref, *rest):
    firsts, seconds, out_ref = rest[:n_dom], rest[n_dom:-1], rest[-1]
    place = order_of(n_dom).index
    pool = paired([firsts[place(k)][...] for k in range(n_dom)], False)
    pool += [far_ref[i] for i in range(n_dom // 2)]
    pool += paired([seconds[place(k)][...] for k in range(n_dom)], False)
    pool = jnp.concatenate(pool, axis=1)
    out_ref[...] = mm(pool, wide_ref[:pool.shape[1], :])


def decode_kernel(n_dom, cols, acc_ref, wide_ref, d2_ref, grid_ref, far_ref, out_ref, buf, sems):
    pool = jnp.concatenate([far_ref[i] for i in range(n_dom // 2)], axis=1)
    dec = silu(acc_ref[...] + mm(pool, wide_ref[wide_ref.shape[0] - pool.shape[1]:, :])).astype(BF)
    copies = []
    for t in range(grid_ref.shape[1] // cols):
        here = slice(t * cols, (t + 1) * cols)
        buf[:, here] = (grid_ref[:, here].astype(F32) + mt(d2_ref[...], dec[:, here])).astype(BF)
        copies.append(pltpu.make_async_copy(
            buf.at[:, pl.ds(t * cols, cols)], out_ref.at[:, pl.ds(t * cols, cols)], sems.at[t]
        ))
        copies[t].start()
    for copy in copies:
        copy.wait()


def order_of(n_dom):
    return [0] + list(range(n_dom // 2, n_dom)) + list(range(1, n_dom // 2))


def move(chunks, n_dom):
    moved = {0: chunks[0]}
    for k in order_of(n_dom)[1:]:
        moved[k] = lax.ppermute(chunks[k], "dom", [(i, i ^ k) for i in range(n_dom)])
    return [moved[k] for k in range(n_dom)]


def local(n_dom, n_feat, grid_state, mesh_state, enc_first, enc_second, dec_first, dec_second,
          mesh_weight, send_grid, enc_tiles, enc_target, send_mesh, dec_slots, dec_tiles):
    rows = grid_state.shape[0]
    block = dec_tiles.shape[1]
    grid_cols = grid_state.shape[1]
    grid_blocks = grid_cols // block
    mesh_cols = mesh_state.shape[1]
    mesh_blocks = mesh_cols // block
    slots = enc_target.shape[-1]
    feeding = dec_slots.shape[1]
    pair = 2 * block
    at = jnp.stack([lax.axis_index("dom"), lax.axis_index("feat"), lax.axis_index("sub")]).astype(jnp.int32)
    send_grid = send_grid.reshape(slots // 2, 2).T
    send_mesh = send_mesh.reshape(slots // 2, 2).T
    chunk = jax.ShapeDtypeStruct((2, rows, pair), BF)
    call = functools.partial(pl.pallas_call, compiler_params=params(12 if n_dom <= 4 else 48))

    out = pl.pallas_call(
        functools.partial(pack_kernel, grid_blocks, n_dom),
        out_shape=[chunk] * n_dom,
        in_specs=[full(SMEM), full(SMEM), anywhere()],
        out_specs=[full()] * n_dom,
        scratch_shapes=[VMEM((rows, grid_cols), BF), VMEM((2, rows, grid_cols + pair), BF), pltpu.SemaphoreType.DMA((4,))],
        cost_estimate=cost(1),
        compiler_params=params(52),
        name="pack",
    )(at, send_grid, grid_state)
    near = move(out, n_dom)

    def whole(w):
        return lax.all_gather(w, "feat", axis=0, tiled=True)

    def cross(kernel, count, chunks, *waits):
        mine = call(
            functools.partial(kernel, n_dom, len(waits)),
            out_shape=jax.ShapeDtypeStruct((count, rows, pair), BF),
            in_specs=[full()] * n_dom + [anywhere()] * len(waits),
            out_specs=full(),
            cost_estimate=cost(0),
            name="stack",
        )(*[chunks[k] for k in order_of(n_dom)], *waits)
        return lax.ppermute(mine, "sub", SWAP), mine

    def rows_of(w):
        return [w, lax.ppermute(w, "feat", SWAP)] if n_feat == 2 else [whole(w)]

    w1, w2, mw = rows_of(enc_first), rows_of(enc_second), whole(mesh_weight)
    to_mesh, split_state = call(
        functools.partial(scatter_kernel, n_dom, mesh_blocks),
        out_shape=[
            jax.ShapeDtypeStruct((2, n_dom * pair, mesh_cols), BF),
            jax.ShapeDtypeStruct(mesh_state.shape, BF),
        ],
        in_specs=[full(SMEM), full(SMEM), full(), full()],
        out_specs=[full(), full()],
        cost_estimate=cost(0),
        name="scatter",
    )(at, enc_target.reshape(slots), enc_tiles.reshape(block, slots * block), mesh_state)
    to_grid = call(
        functools.partial(spread_kernel, n_dom, feeding),
        grid=(grid_blocks // 2,),
        out_shape=jax.ShapeDtypeStruct((slots * block, grid_cols), BF),
        in_specs=[full(SMEM), full(SMEM), pl.BlockSpec((2, block, feeding * block), lambda i: (i, 0, 0))],
        out_specs=pl.BlockSpec((slots * block, pair), lambda i: (0, i)),
        cost_estimate=cost(0),
        name="spread",
    )(at, dec_slots.T, dec_tiles)

    d1 = whole(dec_first)
    far, _ = cross(stack_kernel, n_dom, near, w1[-1], w2[-1], mw, d1, to_mesh)
    acc = call(
        functools.partial(encode_kernel, n_dom),
        out_shape=jax.ShapeDtypeStruct((rows, mesh_cols), F32),
        in_specs=[full(SMEM)] + [full()] * (1 + n_dom + len(w1)),
        out_specs=full(),
        cost_estimate=cost(0.5),
        name="encode",
    )(at, to_mesh, *[near[k] for k in order_of(n_dom)], *w1)
    half = jax.ShapeDtypeStruct((rows, mesh_cols // 2), BF)
    sums = jax.ShapeDtypeStruct((rows, mesh_cols // 2), F32)
    g_first, first, later = call(
        functools.partial(gather_kernel, n_dom),
        out_shape=[sums, half, half],
        in_specs=[full(SMEM)] + [full()] * (4 + len(w1) + len(w2)),
        out_specs=[full()] * 3,
        cost_estimate=cost(0.5),
        name="gather",
    )(at, acc, to_mesh, split_state, far, *w1, *w2)
    g_second, second = call(
        later_kernel,
        out_shape=[sums, half],
        in_specs=[full(SMEM)] + [full()] * (2 + len(w2)),
        out_specs=[full()] * 2,
        cost_estimate=cost(0.5),
        name="later",
    )(at, later, split_state, *w2)

    def other_feat(x):
        if n_feat == 2:
            return lax.ppermute(x, "feat", SWAP)
        return (lax.psum(x.astype(F32), "feat") - x.astype(F32)).astype(BF)

    thin = jax.ShapeDtypeStruct((rows, pair), BF)
    scratch = [VMEM((4, rows, mesh_cols // 2 + pair), BF)]
    *out, second = call(
        functools.partial(first_mesh_kernel, mesh_blocks, n_dom),
        out_shape=[thin] * n_dom + [half],
        in_specs=[full(SMEM), full(SMEM)] + [full()] * 5 + [anywhere()],
        out_specs=[full()] * (n_dom + 1),
        scratch_shapes=scratch,
        cost_estimate=cost(0.5),
        name="mesh",
    )(at, send_mesh, g_first, other_feat(first), mw, d1, second, to_grid)
    near_first = move(out, n_dom)
    out = call(
        functools.partial(mesh_kernel, mesh_blocks, n_dom),
        out_shape=[thin] * n_dom,
        in_specs=[full(SMEM), full(SMEM)] + [full()] * 4,
        out_specs=[full()] * n_dom,
        scratch_shapes=scratch,
        cost_estimate=cost(0.5),
        name="mesh",
    )(at, send_mesh, g_second, other_feat(second), mw, d1)
    near_second = move(out, n_dom)
    d2 = whole(call(
        hold_kernel,
        out_shape=jax.ShapeDtypeStruct(dec_second.shape, BF),
        in_specs=[anywhere(), full()],
        out_specs=full(),
        cost_estimate=cost(0),
        name="hold",
    )(out[0], dec_second))
    ordered = order_of(n_dom)
    far_first, _ = cross(join_kernel, n_dom // 2, near_first, out[0], d2)
    far_second, ready = cross(join_kernel, n_dom // 2, near_second)
    acc = call(
        functools.partial(collect_kernel, n_dom),
        out_shape=jax.ShapeDtypeStruct((rows, grid_cols), F32),
        in_specs=[anywhere()] + [full()] * (2 + 2 * n_dom),
        out_specs=full(),
        cost_estimate=cost(0.5),
        name="collect",
    )(ready, to_grid, far_first, *[near_first[k] for k in ordered], *[near_second[k] for k in ordered])
    return call(
        functools.partial(decode_kernel, n_dom, grid_cols // 3),
        out_shape=jax.ShapeDtypeStruct(grid_state.shape, BF),
        in_specs=[full()] * 5,
        out_specs=anywhere(),
        scratch_shapes=[VMEM((rows, grid_cols), BF), pltpu.SemaphoreType.DMA((3,))],
        cost_estimate=cost(3),
        name="decode",
    )(acc, to_grid, d2, grid_state, far_second)


def solution(mesh):
    whole = ("ens", "dom", "sub", "feat")
    share = ("ens", "dom", "sub")
    in_specs = (
        P(None, whole),
        P("feat", share),
        P("feat", None),
        P("feat", None),
        P("feat", None),
        P("feat", None),
        P("feat", None),
        P(share, "feat", None, None),
        P(share, "feat", None, None),
        P(share, "feat", None),
        P(share, "feat", None, None),
        P(whole, None),
        P(whole, None, None),
    )
    return jax.shard_map(
        functools.partial(local, mesh.shape["dom"], mesh.shape["feat"]),
        mesh=mesh, in_specs=in_specs, out_specs=P(None, whole), check_vma=False,
    )
```

```python
import functools

import jax
import jax.numpy as jnp
from jax import lax
from jax.experimental import pallas as pl
from jax.experimental.pallas import tpu as pltpu
from jax.sharding import PartitionSpec as P

BF = jnp.bfloat16
F32 = jnp.float32
VMEM = pltpu.VMEM
SMEM = pltpu.SMEM
SWAP = [(0, 1), (1, 0)]


def full(space=VMEM):
    return pl.BlockSpec(memory_space=space)


def params(mib):
    return pltpu.CompilerParams(vmem_limit_bytes=int(mib * 1024 * 1024))


def cost(us):
    return pl.CostEstimate(flops=int(us * 4e8), bytes_accessed=int(us * 1e6), transcendentals=0)


def anywhere():
    return pl.BlockSpec(memory_space=pl.ANY)


def silu(x):
    half = 0.5 * x
    return half + half * jnp.tanh(half)


def mm(a, b):
    return jnp.dot(a, b, preferred_element_type=F32)


def mt(w, x):
    return lax.dot_general(w, x, (((0,), (0,)), ((), ())), preferred_element_type=F32)


def turn(v):
    return v.astype(F32).T.astype(BF)


def swap_halves(v, width):
    return jnp.concatenate([v[:, width:], v[:, :width]], axis=1)


def pack_rows(step, blocks, n_dom, at_ref, send_ref, src_ref, buf, i, outs):
    pair = outs[0].shape[2]
    width = pair // 2
    cols = blocks * width
    here = slice(i * step, (i + 1) * step)
    for p in range(blocks // 2):
        v = src_ref[here, p * pair:(p + 1) * pair]
        buf[0, here, p * pair:(p + 1) * pair] = v
        buf[1, here, p * pair:(p + 1) * pair] = swap_halves(v, width)
    low = lax.broadcasted_iota(jnp.int32, (step, pair), 1) < width
    for k in range(n_dom):
        for j in range(2):
            peer = (at_ref[0] ^ k) * 2 + (at_ref[2] ^ j)
            vs = []
            for c in range(2):
                b = send_ref[c, peer]
                used = b < blocks
                start = pl.multiple_of(jnp.where(used, b // 2 * pair, cols), pair)
                flip = jnp.where(used & (lax.rem(b, 2) != c), 1, 0)
                vs.append(buf[flip, here, pl.ds(start, pair)])
            outs[k][j, here, :] = jnp.where(low, vs[0], vs[1])


def pack_kernel(blocks, n_dom, at_ref, send_ref, src_ref, *refs):
    outs, src, buf, sems = refs[:n_dom], refs[n_dom], refs[n_dom + 1], refs[n_dom + 2]
    rows, cols = src_ref.shape
    parts = 4
    step = rows // parts
    copies = []
    for i in range(parts):
        here = pl.ds(i * step, step)
        copies.append(pltpu.make_async_copy(src_ref.at[here, :], src.at[here, :], sems.at[i]))
        copies[i].start()
    buf[0, :, cols:] = jnp.zeros((rows, buf.shape[2] - cols), BF)
    for i in range(parts):
        copies[i].wait()
        pack_rows(step, blocks, n_dom, at_ref, send_ref, src, buf, i, outs)


def stack_kernel(n_dom, waits, *refs):
    chunks, out = refs[:n_dom], refs[n_dom + waits]
    for i, k in enumerate(order_of(n_dom)):
        out[k] = chunks[i][1]


def joined(at_ref, refs):
    if len(refs) == 1:
        return refs[0][...]
    own, got = refs[0][...], refs[1][...]
    first = at_ref[1] == 0
    return jnp.concatenate([jnp.where(first, own, got), jnp.where(first, got, own)], axis=0)


def scatter_kernel(n_dom, mesh_blocks, at_ref, tgt_ref, tiles_ref, ms_ref, out_ref, split_ref):
    block = tiles_ref.shape[0]
    pair, part = 2 * block, block // 2
    wide = mesh_blocks * part
    group = lax.broadcasted_iota(jnp.int32, (1, pair), 1) // part
    for j in range(2):
        for k in range(n_dom):
            peer = (at_ref[0] ^ k) * 2 + (at_ref[2] ^ j)
            t = turn(tiles_ref[:, pl.ds(pl.multiple_of(peer * pair, pair), pair)])
            for h in range(2):
                spread = jnp.concatenate([t[:, h * part:(h + 1) * part]] * 4, axis=1)
                for c in range(2):
                    m = tgt_ref[peer * 2 + c]
                    row = k * pair + c * block
                    for p in range(mesh_blocks // 4):
                        mask = (group + 4 * p == m).astype(F32).astype(BF)
                        at = h * wide + p * pair
                        out_ref[j, row:row + block, at:at + pair] = spread[c * block:(c + 1) * block] * mask
    ms = ms_ref[...]
    for h in range(2):
        for p in range(mesh_blocks // 4):
            split_ref[:, h * wide + p * pair:h * wide + (p + 1) * pair] = jnp.concatenate(
                [ms[:, m * block + h * part:m * block + (h + 1) * part] for m in range(4 * p, 4 * p + 4)], axis=1
            )


def spread_kernel(n_dom, feeding, at_ref, slot_ref, tiles_ref, out_ref):
    g = pl.program_id(0)
    block = tiles_ref.shape[1]
    t = turn(tiles_ref[...].reshape(2 * block, feeding * block))
    half = block // 2
    low = lax.broadcasted_iota(jnp.int32, (half, 2 * block), 1) < block
    out_ref[...] = jnp.zeros_like(out_ref)
    for h in range(2):
        for i in range(feeding):
            q = slot_ref[i, g * 2 + h]
            peer = q // 2
            k = at_ref[0] ^ (peer // 2)
            j = at_ref[2] ^ lax.rem(peer, 2)
            for part in range(2):
                row = part * (out_ref.shape[0] // 2) + ((j * n_dom + k) * 2 + lax.rem(q, 2)) * half
                v = t[i * block + part * half:i * block + (part + 1) * half, :]
                v = jnp.where(low if h == 0 else ~low, v, jnp.zeros_like(v))
                out_ref[pl.ds(pl.multiple_of(row, half), half), :] += v


def encode_kernel(n_dom, at_ref, wide_ref, *rest):
    chunks, ws, out_ref = rest[:n_dom], rest[n_dom:-1], rest[-1]
    place = order_of(n_dom).index
    x = jnp.concatenate([chunks[place(k)][0] for k in range(n_dom)], axis=1)
    hid = silu(mt(joined(at_ref, ws), x)).astype(BF)
    out_ref[...] = mm(hid, wide_ref[0])


def messages(at_ref, ws, h, total, ms_ref, g_ref, out_ref):
    g_ref[...] = mt(joined(at_ref, ws), total)
    rows = ms_ref.shape[0]
    cols = g_ref.shape[1]
    here = pl.ds(pl.multiple_of(at_ref[1] * rows, rows), rows)
    g_ref[here, :] += ms_ref[:, h * cols:(h + 1) * cols].astype(F32)
    out_ref[...] = g_ref[...].astype(BF)


def gather_kernel(n_dom, at_ref, acc_ref, wide_ref, ms_ref, far_ref, *rest):
    ws, (g_ref, first_ref, later_ref) = rest[:-3], rest[-3:]
    count = len(ws) // 2
    half = g_ref.shape[1]
    x = jnp.concatenate([far_ref[k] for k in range(n_dom)], axis=1)
    hid = silu(mt(joined(at_ref, ws[:count]), x)).astype(BF)
    total = (acc_ref[...] + mm(hid, wide_ref[1])).astype(BF)
    messages(at_ref, ws[count:], 0, total[:, :half], ms_ref, g_ref, first_ref)
    later_ref[...] = total[:, half:]


def later_kernel(at_ref, total_ref, ms_ref, *rest):
    ws, (g_ref, out_ref) = rest[:-2], rest[-2:]
    messages(at_ref, ws, 1, total_ref[...], ms_ref, g_ref, out_ref)


def mesh_kernel(blocks, n_dom, at_ref, send_ref, g_ref, other_ref, mw_ref, d1_ref, *rest):
    outs, buf = rest[-1 - n_dom:-1], rest[-1]
    rows = g_ref.shape[0]
    cols = g_ref.shape[1]
    new = (g_ref[...] + other_ref[...].astype(F32)).astype(BF)
    hid = silu(mt(mw_ref[...], new)).astype(BF)
    hid = mt(d1_ref[...], hid).astype(BF)
    part = cols // blocks
    for p in range(cols // 128):
        v = hid[:, p * 128:(p + 1) * 128]
        buf[0, :, p * 128:(p + 1) * 128] = v
        for turned in range(1, 4):
            cut = 128 - turned * part
            buf[turned, :, p * 128:(p + 1) * 128] = jnp.concatenate([v[:, cut:], v[:, :cut]], axis=1)
    buf[0, :, cols:] = jnp.zeros((rows, 128), BF)
    step = rows // 4
    group = lax.broadcasted_iota(jnp.int32, (step, 128), 1) // part
    for k in range(n_dom):
        picks = []
        for i in range(4):
            b = send_ref[i % 2, (at_ref[0] ^ k) * 2 + (at_ref[2] ^ (i // 2))]
            used = b < blocks
            start = pl.multiple_of(jnp.where(used, b // 4 * 128, cols), 128)
            picks.append((jnp.where(used, lax.rem(i + 4 - lax.rem(b, 4), 4), 0), start))
        for r in range(4):
            here = slice(r * step, (r + 1) * step)
            vs = [buf[turned, here, pl.ds(start, 128)] for turned, start in picks]
            outs[k][here, :] = jnp.where(
                group < 2, jnp.where(group == 0, vs[0], vs[1]), jnp.where(group == 2, vs[2], vs[3])
            )


def after_kernel(blocks, n_dom, ready_ref, *refs):
    mesh_kernel(blocks, n_dom, *refs)


def hold_kernel(ready_ref, x_ref, out_ref):
    out_ref[...] = x_ref[...]


def paired(chunks, upper):
    width = chunks[0].shape[1] // 2
    low = lax.broadcasted_iota(jnp.int32, chunks[0].shape, 1) < width
    out = []
    for a, b in zip(chunks[::2], chunks[1::2]):
        a, b = (swap_halves(a, width), b) if upper else (a, swap_halves(b, width))
        out.append(jnp.where(low, a, b))
    return out


def join_kernel(n_dom, waits, *refs):
    chunks, out = refs[:n_dom], refs[n_dom + waits]
    place = order_of(n_dom).index
    for i, v in enumerate(paired([chunks[place(k)][...] for k in range(n_dom)], True)):
        out[i] = v


def collect_kernel(n_dom, ready_ref, wide_ref, far_ref, *rest):
    firsts, seconds, out_ref = rest[:n_dom], rest[n_dom:-1], rest[-1]
    place = order_of(n_dom).index
    pool = paired([firsts[place(k)][...] for k in range(n_dom)], False)
    pool += [far_ref[i] for i in range(n_dom // 2)]
    pool += paired([seconds[place(k)][...] for k in range(n_dom)], False)
    pool = jnp.concatenate(pool, axis=1)
    out_ref[...] = mm(pool, wide_ref[:pool.shape[1], :])


def decode_kernel(n_dom, cols, acc_ref, wide_ref, d2_ref, grid_ref, far_ref, out_ref, buf, sems):
    pool = jnp.concatenate([far_ref[i] for i in range(n_dom // 2)], axis=1)
    dec = silu(acc_ref[...] + mm(pool, wide_ref[wide_ref.shape[0] - pool.shape[1]:, :])).astype(BF)
    copies = []
    for t in range(grid_ref.shape[1] // cols):
        here = slice(t * cols, (t + 1) * cols)
        buf[:, here] = (grid_ref[:, here].astype(F32) + mt(d2_ref[...], dec[:, here])).astype(BF)
        copies.append(pltpu.make_async_copy(
            buf.at[:, pl.ds(t * cols, cols)], out_ref.at[:, pl.ds(t * cols, cols)], sems.at[t]
        ))
        copies[t].start()
    for copy in copies:
        copy.wait()


def order_of(n_dom):
    return [0] + list(range(n_dom // 2, n_dom)) + list(range(1, n_dom // 2))


def move(chunks, n_dom):
    moved = {0: chunks[0]}
    for k in order_of(n_dom)[1:]:
        moved[k] = lax.ppermute(chunks[k], "dom", [(i, i ^ k) for i in range(n_dom)])
    return [moved[k] for k in range(n_dom)]


def local(n_dom, n_feat, grid_state, mesh_state, enc_first, enc_second, dec_first, dec_second,
          mesh_weight, send_grid, enc_tiles, enc_target, send_mesh, dec_slots, dec_tiles):
    rows = grid_state.shape[0]
    block = dec_tiles.shape[1]
    grid_cols = grid_state.shape[1]
    grid_blocks = grid_cols // block
    mesh_cols = mesh_state.shape[1]
    mesh_blocks = mesh_cols // block
    slots = enc_target.shape[-1]
    feeding = dec_slots.shape[1]
    pair = 2 * block
    at = jnp.stack([lax.axis_index("dom"), lax.axis_index("feat"), lax.axis_index("sub")]).astype(jnp.int32)
    send_grid = send_grid.reshape(slots // 2, 2).T
    send_mesh = send_mesh.reshape(slots // 2, 2).T
    chunk = jax.ShapeDtypeStruct((2, rows, pair), BF)
    call = functools.partial(pl.pallas_call, compiler_params=params(12 if n_dom <= 4 else 48))

    out = pl.pallas_call(
        functools.partial(pack_kernel, grid_blocks, n_dom),
        out_shape=[chunk] * n_dom,
        in_specs=[full(SMEM), full(SMEM), anywhere()],
        out_specs=[full()] * n_dom,
        scratch_shapes=[VMEM((rows, grid_cols), BF), VMEM((2, rows, grid_cols + pair), BF), pltpu.SemaphoreType.DMA((4,))],
        cost_estimate=cost(1),
        compiler_params=params(52),
        name="pack",
    )(at, send_grid, grid_state)
    near = move(out, n_dom)

    def whole(w):
        return lax.all_gather(w, "feat", axis=0, tiled=True)

    def cross(kernel, count, chunks, *waits):
        mine = call(
            functools.partial(kernel, n_dom, len(waits)),
            out_shape=jax.ShapeDtypeStruct((count, rows, pair), BF),
            in_specs=[full()] * n_dom + [anywhere()] * len(waits),
            out_specs=full(),
            cost_estimate=cost(0),
            name="stack",
        )(*[chunks[k] for k in order_of(n_dom)], *waits)
        return lax.ppermute(mine, "sub", SWAP), mine

    def rows_of(w):
        return [w, lax.ppermute(w, "feat", SWAP)] if n_feat == 2 else [whole(w)]

    w1, w2, mw = rows_of(enc_first), rows_of(enc_second), whole(mesh_weight)
    to_mesh, split_state = call(
        functools.partial(scatter_kernel, n_dom, mesh_blocks),
        out_shape=[
            jax.ShapeDtypeStruct((2, n_dom * pair, mesh_cols), BF),
            jax.ShapeDtypeStruct(mesh_state.shape, BF),
        ],
        in_specs=[full(SMEM), full(SMEM), full(), full()],
        out_specs=[full(), full()],
        cost_estimate=cost(0),
        name="scatter",
    )(at, enc_target.reshape(slots), enc_tiles.reshape(block, slots * block), mesh_state)
    to_grid = call(
        functools.partial(spread_kernel, n_dom, feeding),
        grid=(grid_blocks // 2,),
        out_shape=jax.ShapeDtypeStruct((slots * block, grid_cols), BF),
        in_specs=[full(SMEM), full(SMEM), pl.BlockSpec((2, block, feeding * block), lambda i: (i, 0, 0))],
        out_specs=pl.BlockSpec((slots * block, pair), lambda i: (0, i)),
        cost_estimate=cost(0),
        name="spread",
    )(at, dec_slots.T, dec_tiles)

    d1 = whole(dec_first)
    far, _ = cross(stack_kernel, n_dom, near, w1[-1], w2[-1], mw, d1, to_mesh)
    acc = call(
        functools.partial(encode_kernel, n_dom),
        out_shape=jax.ShapeDtypeStruct((rows, mesh_cols), F32),
        in_specs=[full(SMEM)] + [full()] * (1 + n_dom + len(w1)),
        out_specs=full(),
        cost_estimate=cost(0.5),
        name="encode",
    )(at, to_mesh, *[near[k] for k in order_of(n_dom)], *w1)
    half = jax.ShapeDtypeStruct((rows, mesh_cols // 2), BF)
    sums = jax.ShapeDtypeStruct((rows, mesh_cols // 2), F32)
    g_first, first, later = call(
        functools.partial(gather_kernel, n_dom),
        out_shape=[sums, half, half],
        in_specs=[full(SMEM)] + [full()] * (4 + len(w1) + len(w2)),
        out_specs=[full()] * 3,
        cost_estimate=cost(0.5),
        name="gather",
    )(at, acc, to_mesh, split_state, far, *w1, *w2)
    g_second, second = call(
        later_kernel,
        out_shape=[sums, half],
        in_specs=[full(SMEM)] + [full()] * (2 + len(w2)),
        out_specs=[full()] * 2,
        cost_estimate=cost(0.5),
        name="later",
    )(at, later, split_state, *w2)

    def other_feat(x):
        if n_feat == 2:
            return lax.ppermute(x, "feat", SWAP)
        return (lax.psum(x.astype(F32), "feat") - x.astype(F32)).astype(BF)

    thin = jax.ShapeDtypeStruct((rows, pair), BF)
    scratch = [VMEM((4, rows, mesh_cols // 2 + pair), BF)]
    out = call(
        functools.partial(after_kernel, mesh_blocks, n_dom),
        out_shape=[thin] * n_dom,
        in_specs=[anywhere(), full(SMEM), full(SMEM)] + [full()] * 4,
        out_specs=[full()] * n_dom,
        scratch_shapes=scratch,
        cost_estimate=cost(0.5),
        name="mesh",
    )(to_grid, at, send_mesh, g_first, other_feat(first), mw, d1)
    near_first = move(out, n_dom)
    out = call(
        functools.partial(after_kernel, mesh_blocks, n_dom),
        out_shape=[thin] * n_dom,
        in_specs=[anywhere(), full(SMEM), full(SMEM)] + [full()] * 4,
        out_specs=[full()] * n_dom,
        scratch_shapes=scratch,
        cost_estimate=cost(0.5),
        name="mesh",
    )(out[0], at, send_mesh, g_second, other_feat(second), mw, d1)
    near_second = move(out, n_dom)
    d2 = whole(call(
        hold_kernel,
        out_shape=jax.ShapeDtypeStruct(dec_second.shape, BF),
        in_specs=[anywhere(), full()],
        out_specs=full(),
        cost_estimate=cost(0),
        name="hold",
    )(out[0], dec_second))
    ordered = order_of(n_dom)
    far_first, _ = cross(join_kernel, n_dom // 2, near_first, out[0], d2)
    far_second, ready = cross(join_kernel, n_dom // 2, near_second)
    acc = call(
        functools.partial(collect_kernel, n_dom),
        out_shape=jax.ShapeDtypeStruct((rows, grid_cols), F32),
        in_specs=[anywhere()] + [full()] * (2 + 2 * n_dom),
        out_specs=full(),
        cost_estimate=cost(0.5),
        name="collect",
    )(ready, to_grid, far_first, *[near_first[k] for k in ordered], *[near_second[k] for k in ordered])
    return call(
        functools.partial(decode_kernel, n_dom, grid_cols // 3),
        out_shape=jax.ShapeDtypeStruct(grid_state.shape, BF),
        in_specs=[full()] * 5,
        out_specs=anywhere(),
        scratch_shapes=[VMEM((rows, grid_cols), BF), pltpu.SemaphoreType.DMA((3,))],
        cost_estimate=cost(3),
        name="decode",
    )(acc, to_grid, d2, grid_state, far_second)


def solution(mesh):
    whole = ("ens", "dom", "sub", "feat")
    share = ("ens", "dom", "sub")
    in_specs = (
        P(None, whole),
        P("feat", share),
        P("feat", None),
        P("feat", None),
        P("feat", None),
        P("feat", None),
        P("feat", None),
        P(share, "feat", None, None),
        P(share, "feat", None, None),
        P(share, "feat", None),
        P(share, "feat", None, None),
        P(whole, None),
        P(whole, None, None),
    )
    return jax.shard_map(
        functools.partial(local, mesh.shape["dom"], mesh.shape["feat"]),
        mesh=mesh, in_specs=in_specs, out_specs=P(None, whole), check_vma=False,
    )
```
